128 devices in a mesh: dp: 8 (over y_hi, x), seq: 16 (over y_lo, z, core).
Axes of the slice: x: 4, y: 4 (y_hi: 2, y_lo: 2; y = y_hi * 2 + y_lo), z: 4, core: 2. Of those that a mesh axis runs over, the one named last changes fastest.
Arguments:
- layer_input: bfloat16 [8, 32, 256, 1152], P('dp', 'seq'), may hold values from -6 to 6
- cotangent: bfloat16 [8, 32, 256, 1152], P('dp', 'seq'), may hold values from -6 to 6
- spatial_qkv: bfloat16 [1152, 3456], replicated, may hold values from -1 to 1
- spatial_out: bfloat16 [1152, 1152], replicated, may hold values from -0.1875 to 0.1875
- temporal_qkv: bfloat16 [1152, 3456], replicated, may hold values from -1 to 1
- temporal_out: bfloat16 [1152, 1152], replicated, may hold values from -0.1875 to 0.1875
Outputs:
- input_grad: bfloat16 [8, 32, 256, 1152], P('dp', 'seq')
- spatial_out_grad: float32 [1152, 1152], P('seq')
- temporal_out_grad: float32 [1152, 1152], P('seq')
The draws below stay inside these ranges and needn't reach their ends.
All inputs are finite; a program needn't handle non-finite values.
Results may differ from the reference program's by a relative error of at most 0.03.
Values may be sent and summed in bfloat16 or wider, within the bound.
A program may use at most 192 MiB of HBM per device.

```python
import math
import jax
import jax.numpy as jnp
from jax import lax

D = 1152
HEADS = 16
HW = 256
FRAMES = 32
CLIPS = 8
ALL_TOKENS = 65536


def qkv_weights(seed_key, top_gain):
    base_key = jax.random.fold_in(seed_key, 0)
    gain_key = jax.random.fold_in(seed_key, 2)
    base = jax.random.normal(base_key, (D, 3 * D), jnp.float32) / math.sqrt(D)
    head_gain = jnp.exp(jax.random.uniform(gain_key, (HEADS,), jnp.float32, math.log(0.5), math.log(top_gain)))
    column_gain = jnp.repeat(head_gain, D // HEADS)
    queries = base[:, :D] * column_gain
    key_rows = base[:, D:2 * D] * column_gain
    values = base[:, 2 * D:]
    joined = jnp.concatenate([queries, key_rows, values], axis=1)
    return jnp.clip(joined, -1.0, 1.0).astype(jnp.bfloat16)


def draw_spatial_qkv(key, part):
    key = jax.random.fold_in(key, 17)
    return qkv_weights(key, 1.0)


def draw_temporal_qkv(key, part):
    key = jax.random.fold_in(key, 29)
    return qkv_weights(key, 1.0)


def levels(rng, shape, cuts, least, top_value):
    factor_of, own = 1.0, jax.random.fold_in(rng, 6)
    for position, blocks in cuts:
        heights = jnp.exp(jax.random.uniform(jax.random.fold_in(own, position), (blocks,), jnp.float32, least / len(cuts), top_value / len(cuts)))
        factor_of = factor_of * jnp.repeat(heights, shape[position] // blocks).reshape([-1 if axis == position else 1 for axis in range(len(shape))])
    return factor_of


def centred(stream_key, shape, spread, reach, cuts=(), dtype=jnp.bfloat16):
    values = jax.random.normal(stream_key, shape, jnp.float32) * spread
    if len(cuts) > 0:
        values = levels(stream_key, shape, cuts, -0.22, 0.18) * values
    return jnp.clip(values, min=-reach, max=reach).astype(dtype)


def setup_inputs(seed: int = 0) -> dict:
    seeds = jax.random.split(jax.random.key(seed), 7)
    return {
        "layer_input": centred(seeds[0], (CLIPS, FRAMES, HW, D), 1.0, 6.0, ((0, 8), (1, 16))),
        "cotangent": centred(seeds[1], (CLIPS, FRAMES, HW, D), 1.0, 6.0, ((0, 8), (1, 16))),
        "spatial_qkv": draw_spatial_qkv(jax.random.fold_in(seeds[6], 71), 0),
        "spatial_out": centred(seeds[3], (D, D), D ** -0.5, 0.1875),
        "temporal_qkv": draw_temporal_qkv(jax.random.fold_in(seeds[6], 71), 0),
        "temporal_out": centred(seeds[5], (D, D), D ** -0.5, 0.1875),
    }


EPSILON = 1e-06
SPATIAL_FORMS = ('bflhe,bfmhe->bfhlm', 'bfhlm,bfmhe->bflhe', 'bfhlm,bflhe->bfmhe')
TEMPORAL_FORMS = ('blphe,bmphe->bphlm', 'bphlm,bmphe->blphe', 'bphlm,blphe->bmphe')

def widen(array):
    return lax.optimization_barrier(array).astype(jnp.float32)

def rms_forward(block):
    widened = block.astype(jnp.float32)
    inverse_rms = lax.rsqrt(lax.optimization_barrier(jnp.mean(widened * widened, axis=-1, keepdims=True)) + EPSILON)
    return ((widened * inverse_rms).astype(jnp.bfloat16), inverse_rms)

def rms_backward(block, grad_norm, inverse_rms):
    widened = block.astype(jnp.float32)
    grad_wide = grad_norm.astype(jnp.float32)
    inner = lax.optimization_barrier(jnp.mean(grad_wide * widened, axis=-1, keepdims=True))
    return inverse_rms * grad_wide - widened * inverse_rms * inverse_rms * inverse_rms * inner

def project(block, weight):
    return jnp.dot(block, weight, preferred_element_type=jnp.float32)

def project_back(block, weight):
    return lax.dot_general(block, weight, (((block.ndim - 1,), (1,)), ((), ())), preferred_element_type=jnp.float32)

def split_heads(packed, count):
    width = packed.shape[-1] // count
    pieces = []
    for index in range(count):
        piece = packed[..., index * width:(index + 1) * width]
        pieces.append(piece.reshape(packed.shape[:-1] + (HEADS, width // HEADS)))
    return pieces

def join_heads(heads_array):
    return heads_array.reshape(heads_array.shape[:-2] + (heads_array.shape[-2] * heads_array.shape[-1],))

def attend(queries, key_rows, values, forms):
    score_scale = 1.0 / math.sqrt(queries.shape[-1])
    scores = jnp.einsum(forms[0], widen(queries), widen(key_rows)) * score_scale
    attention = jax.nn.softmax(scores, axis=-1)
    mixed = jnp.einsum(forms[1], widen(attention.astype(jnp.bfloat16)), widen(values))
    return (mixed.astype(jnp.bfloat16), attention)

def attend_back(queries, key_rows, values, attention, grad_mixed, forms):
    score_scale = 1.0 / math.sqrt(queries.shape[-1])
    rounded = widen(attention.astype(jnp.bfloat16))
    grad_values = jnp.einsum(forms[2], rounded, widen(grad_mixed)).astype(jnp.bfloat16)
    grad_attention = jnp.einsum(forms[0], widen(grad_mixed), widen(values))
    inner = lax.optimization_barrier(jnp.sum(attention * grad_attention, axis=-1, keepdims=True))
    grad_scores = (attention * (grad_attention - inner) * score_scale).astype(jnp.bfloat16)
    grad_query = jnp.einsum(forms[1], widen(grad_scores), widen(key_rows)).astype(jnp.bfloat16)
    grad_keys = jnp.einsum(forms[2], widen(grad_scores), widen(queries)).astype(jnp.bfloat16)
    return jnp.concatenate([join_heads(grad_query), join_heads(grad_keys), join_heads(grad_values)], axis=-1)

def row_product(left, right):
    left_rows = left.reshape(-1, left.shape[-1])
    right_rows = right.reshape(-1, right.shape[-1])
    return jnp.dot(left_rows.T, right_rows, preferred_element_type=jnp.float32)

def clip_pass(layer_input, cotangent, spatial_qkv, spatial_out, temporal_qkv, temporal_out):
    norm_one, inverse_one = rms_forward(layer_input)
    packed_one = project(norm_one, spatial_qkv).astype(jnp.bfloat16)
    query_one, keys_one, values_one = split_heads(packed_one, 3)
    mixed_heads, attention_one = attend(query_one, keys_one, values_one, SPATIAL_FORMS)
    mixed_one = join_heads(mixed_heads)
    residual_one = (layer_input.astype(jnp.float32) + project(mixed_one, spatial_out)).astype(jnp.bfloat16)
    norm_two, inverse_two = rms_forward(residual_one)
    packed_two = project(norm_two, temporal_qkv).astype(jnp.bfloat16)
    query_two, keys_two, values_two = split_heads(packed_two, 3)
    mixed_heads_two, attention_two = attend(query_two, keys_two, values_two, TEMPORAL_FORMS)
    mixed_two = join_heads(mixed_heads_two)
    grad_mixed_two = project_back(cotangent, temporal_out).astype(jnp.bfloat16)
    grad_heads_two = split_heads(grad_mixed_two, 1)[0]
    grad_packed_two = attend_back(query_two, keys_two, values_two, attention_two, grad_heads_two, TEMPORAL_FORMS)
    grad_norm_two = project_back(grad_packed_two, temporal_qkv).astype(jnp.bfloat16)
    grad_residual = (cotangent.astype(jnp.float32) + rms_backward(residual_one, grad_norm_two, inverse_two)).astype(jnp.bfloat16)
    grad_mixed_one = project_back(grad_residual, spatial_out).astype(jnp.bfloat16)
    grad_heads_one = split_heads(grad_mixed_one, 1)[0]
    grad_packed_one = attend_back(query_one, keys_one, values_one, attention_one, grad_heads_one, SPATIAL_FORMS)
    grad_norm_one = project_back(grad_packed_one, spatial_qkv).astype(jnp.bfloat16)
    input_grad = (grad_residual.astype(jnp.float32) + rms_backward(layer_input, grad_norm_one, inverse_one)).astype(jnp.bfloat16)
    return (input_grad, row_product(mixed_one, grad_residual), row_product(mixed_two, cotangent))

def reference(layer_input, cotangent, spatial_qkv, spatial_out, temporal_qkv, temporal_out):

    def per_clip(pair):
        input_clip, cot_clip = pair
        result = clip_pass(input_clip[None], cot_clip[None], spatial_qkv, spatial_out, temporal_qkv, temporal_out)
        return (result[0][0], result[1], result[2])
    input_grad, spatial_terms, temporal_terms = lax.map(per_clip, (layer_input, cotangent))
    factor = 1.0 / math.sqrt(ALL_TOKENS)
    spatial_out_grad = lax.optimization_barrier(jnp.sum(spatial_terms, axis=0)) * factor
    temporal_out_grad = lax.optimization_barrier(jnp.sum(temporal_terms, axis=0)) * factor
    return (input_grad, spatial_out_grad, temporal_out_grad)
```

```python
import math

import jax
import jax.numpy as jnp
from jax import lax
from jax.sharding import PartitionSpec as P

HEADS = 16


EPSILON = 1e-06
SPATIAL_FORMS = ("bflhe,bfmhe->bfhlm", "bfhlm,bfmhe->bflhe", "bfhlm,bflhe->bfmhe")
TEMPORAL_FORMS = ("blphe,bmphe->bphlm", "bphlm,bmphe->blphe", "bphlm,blphe->bmphe")


def rms_forward(block):
    widened = block.astype(jnp.float32)
    inverse_rms = lax.rsqrt(jnp.mean(widened * widened, axis=-1, keepdims=True) + EPSILON)
    return ((widened * inverse_rms).astype(jnp.bfloat16), inverse_rms)


def rms_backward(block, grad_norm, inverse_rms):
    widened = block.astype(jnp.float32)
    grad_wide = grad_norm.astype(jnp.float32)
    inner = jnp.mean(grad_wide * widened, axis=-1, keepdims=True)
    return inverse_rms * grad_wide - widened * inverse_rms * inverse_rms * inverse_rms * inner


def project(block, weight):
    return jnp.dot(block, weight, preferred_element_type=jnp.float32)


def project_back(block, weight):
    return lax.dot_general(
        block, weight, (((block.ndim - 1,), (1,)), ((), ())), preferred_element_type=jnp.float32
    )


def split_heads(packed, count):
    width = packed.shape[-1] // count
    pieces = []
    for index in range(count):
        piece = packed[..., index * width : (index + 1) * width]
        pieces.append(piece.reshape(packed.shape[:-1] + (HEADS, width // HEADS)))
    return pieces


def join_heads(heads_array):
    return heads_array.reshape(
        heads_array.shape[:-2] + (heads_array.shape[-2] * heads_array.shape[-1],)
    )


def attend(queries, key_rows, values, forms):
    score_scale = 1.0 / math.sqrt(queries.shape[-1])
    scores = (
        jnp.einsum(forms[0], queries, key_rows, preferred_element_type=jnp.float32) * score_scale
    )
    attention = jax.nn.softmax(scores, axis=-1)
    mixed = jnp.einsum(
        forms[1], attention.astype(jnp.bfloat16), values, preferred_element_type=jnp.float32
    )
    return (mixed.astype(jnp.bfloat16), attention)


def attend_back(queries, key_rows, values, attention, grad_mixed, forms):
    score_scale = 1.0 / math.sqrt(queries.shape[-1])
    rounded = attention.astype(jnp.bfloat16)
    grad_values = jnp.einsum(
        forms[2], rounded, grad_mixed, preferred_element_type=jnp.float32
    ).astype(jnp.bfloat16)
    grad_attention = jnp.einsum(forms[0], grad_mixed, values, preferred_element_type=jnp.float32)
    inner = jnp.sum(attention * grad_attention, axis=-1, keepdims=True)
    grad_scores = (attention * (grad_attention - inner) * score_scale).astype(jnp.bfloat16)
    grad_query = jnp.einsum(
        forms[1], grad_scores, key_rows, preferred_element_type=jnp.float32
    ).astype(jnp.bfloat16)
    grad_keys = jnp.einsum(
        forms[2], grad_scores, queries, preferred_element_type=jnp.float32
    ).astype(jnp.bfloat16)
    return jnp.concatenate(
        [join_heads(grad_query), join_heads(grad_keys), join_heads(grad_values)], axis=-1
    )


def temporal_core(packed, cot_rows, temporal_out):
    queries, key_rows, values = split_heads(packed, 3)
    mixed_heads, attention = attend(queries, key_rows, values, TEMPORAL_FORMS)
    grad_mixed = project_back(cot_rows, temporal_out).astype(jnp.bfloat16)
    grad_heads = split_heads(grad_mixed, 1)[0]
    grad_packed = attend_back(queries, key_rows, values, attention, grad_heads, TEMPORAL_FORMS)
    return (grad_packed, join_heads(mixed_heads))


def slice_product(left_rows, right_rows):
    return lax.dot_general(
        left_rows, right_rows, (((0,), (0,)), ((), ())), preferred_element_type=jnp.float32
    )


def reduce_rows(product):
    share = lax.psum_scatter(
        product.astype(jnp.bfloat16), "seq", scatter_dimension=0, tiled=True
    )
    parts = lax.all_gather(share, "dp", axis=0, tiled=False)
    return jnp.sum(parts.astype(jnp.float32), axis=0)


def local(layer_input, cotangent, spatial_qkv, spatial_out, temporal_qkv, temporal_out):
    width = layer_input.shape[-1]
    seq_count = lax.axis_size("seq")
    data_count = lax.axis_size("dp")
    total_tokens = (
        layer_input.shape[0] * layer_input.shape[1] * layer_input.shape[2] * data_count * seq_count
    )
    factor = 1.0 / math.sqrt(total_tokens)
    norm_one, inverse_one = rms_forward(layer_input)
    packed_one = project(norm_one, spatial_qkv).astype(jnp.bfloat16)
    query_one, keys_one, values_one = split_heads(packed_one, 3)
    mixed_heads, attention_one = attend(query_one, keys_one, values_one, SPATIAL_FORMS)
    mixed_one = join_heads(mixed_heads)
    residual_one = (layer_input.astype(jnp.float32) + project(mixed_one, spatial_out)).astype(
        jnp.bfloat16
    )
    cot_pos = lax.all_to_all(cotangent, "seq", split_axis=2, concat_axis=1, tiled=True)
    residual_pos = lax.all_to_all(residual_one, "seq", split_axis=2, concat_axis=1, tiled=True)
    norm_two, inverse_two = rms_forward(residual_pos)
    packed_pos = project(norm_two, temporal_qkv).astype(jnp.bfloat16)
    grad_packed_pos, mixed_two = temporal_core(packed_pos, cot_pos, temporal_out)
    grad_norm_two = project_back(grad_packed_pos, temporal_qkv).astype(jnp.bfloat16)
    grad_residual_pos = (
        cot_pos.astype(jnp.float32) + rms_backward(residual_pos, grad_norm_two, inverse_two)
    ).astype(jnp.bfloat16)
    temporal_left = mixed_two.reshape(-1, width)
    temporal_right = cot_pos.reshape(-1, width)
    temporal_share = reduce_rows(slice_product(temporal_left, temporal_right))
    grad_residual = lax.all_to_all(
        grad_residual_pos, "seq", split_axis=1, concat_axis=2, tiled=True
    )
    spatial_left = mixed_one.reshape(-1, width)
    spatial_right = grad_residual.reshape(-1, width)
    spatial_share = reduce_rows(slice_product(spatial_left, spatial_right))
    grad_mixed_one = project_back(grad_residual, spatial_out).astype(jnp.bfloat16)
    grad_heads_one = split_heads(grad_mixed_one, 1)[0]
    grad_packed_one = attend_back(
        query_one, keys_one, values_one, attention_one, grad_heads_one, SPATIAL_FORMS
    )
    grad_norm_one = project_back(grad_packed_one, spatial_qkv).astype(jnp.bfloat16)
    input_grad = (
        grad_residual.astype(jnp.float32) + rms_backward(layer_input, grad_norm_one, inverse_one)
    ).astype(jnp.bfloat16)
    spatial_out_grad = spatial_share * factor
    temporal_out_grad = temporal_share * factor
    return (input_grad, spatial_out_grad, temporal_out_grad)


def solution(mesh):
    placed = (P("dp", "seq", None, None), P("dp", "seq", None, None), P(), P(), P(), P())
    return jax.shard_map(
        local,
        mesh=mesh,
        in_specs=placed,
        out_specs=(P("dp", "seq", None, None), P("seq", None), P("seq", None)),
        check_vma=False,
    )
```

```python
import functools
import math

import jax
import jax.numpy as jnp
from jax import lax
from jax.experimental import pallas as pl
from jax.experimental.pallas import tpu as pltpu
from jax.sharding import PartitionSpec as P

D = 1152
HEADS = 16
HEAD = D // HEADS
HW = 256
FRAMES = 32
SEQ = 16
DP = 8
TOKENS = 512
SHARE = D // SEQ
PADDED = 80
EPSILON = 1e-06
SCALE = 1.0 / math.sqrt(HEAD)
LOG2_E = math.log2(math.e)
F32 = jnp.float32
BF16 = jnp.bfloat16
MESH = pl.DeviceIdType.MESH
HALF = slice(0, HW)


def nn(left, right):
    return lax.dot_general(left, right, (((1,), (0,)), ((), ())), preferred_element_type=F32)


def nt(left, right):
    return lax.dot_general(left, right, (((1,), (1,)), ((), ())), preferred_element_type=F32)


def tn(left, right):
    return lax.dot_general(left, right, (((0,), (0,)), ((), ())), preferred_element_type=F32)


def chunks(width, step):
    return [(at, min(step, width - at)) for at in range(0, width, step)]


def rms_forward(block):
    widened = block.astype(F32)
    inverse = lax.rsqrt(jnp.mean(widened * widened, axis=-1, keepdims=True) + EPSILON)
    return (widened * inverse).astype(BF16), inverse


def rms_backward(block, grad_norm, inverse):
    widened = block.astype(F32)
    grad_wide = grad_norm.astype(F32)
    inner = jnp.mean(grad_wide * widened, axis=-1, keepdims=True)
    return inverse * grad_wide - widened * (inverse * inverse * inverse * inner)


def one_hot(rows, columns, target):
    row = lax.broadcasted_iota(jnp.int32, (rows, columns), 0)
    column = lax.broadcasted_iota(jnp.int32, (rows, columns), 1)
    return jnp.where(column == target(row), 1.0, 0.0).astype(BF16)


def pair_masks(pair):
    lane = lax.broadcasted_iota(jnp.int32, (1, 256), 1)
    first = (lane >= 16 * pair) & (lane < 16 * pair + HEAD)
    second = (lane >= 16 * pair + HEAD) & (lane < 16 * pair + 2 * HEAD)
    return first, second


def window(pair, base=0):
    return pl.ds(pl.multiple_of(128 * pair + base, 128), 256)


def tile(pair, base=0):
    return pl.ds(pl.multiple_of(128 * pair + base, 128), 128)


def pick(values, mask):
    return jnp.where(mask, values, jnp.zeros_like(values))


def put(ref, rows, base, pair, carry, result):
    ref[rows, tile(pair, base)] = (carry + result[:, :128]).astype(BF16)
    return result[:, 128:]


def softmax_keys(scores):
    top = jnp.max(scores, axis=0, keepdims=True)
    powers = jnp.exp2((scores - top) * (SCALE * LOG2_E))
    return powers * (1.0 / jnp.sum(powers, axis=0, keepdims=True))


def over_pairs(body, outputs):
    zero = jnp.zeros((HW, 128), F32)
    carries = lax.fori_loop(0, HEADS // 2, body, (zero,) * len(outputs), unroll=HEADS // 2)
    for (ref, rows, base), carry in zip(outputs, carries):
        ref[rows, base + 1024 : base + 1152] = carry.astype(BF16)


def spatial_forward(packed, mixed, probs, frame):
    rows = slice(frame * HW, frame * HW + HW)

    def body(pair, carries):
        masks = pair_masks(pair)
        queries = packed[rows, window(pair)]
        keys = packed[rows, window(pair, D)]
        values = packed[rows, window(pair, 2 * D)]
        weights = []
        for index, mask in enumerate(masks):
            weight = softmax_keys(nt(pick(keys, mask), queries)).astype(BF16)
            probs[frame * HEADS + 2 * pair + index] = weight
            weights.append(weight)
        result = tn(
            jnp.concatenate(weights, axis=0),
            jnp.concatenate([pick(values, mask) for mask in masks], axis=0),
        )
        return (put(mixed, rows, 0, pair, carries[0], result),)

    over_pairs(body, [(mixed, rows, 0)])


def spatial_backward(packed, grad_mixed, grad_packed, probs, frame):
    rows = slice(frame * HW, frame * HW + HW)

    def body(pair, carries):
        masks = pair_masks(pair)
        queries = packed[rows, window(pair)]
        keys = packed[rows, window(pair, D)]
        values = packed[rows, window(pair, 2 * D)]
        grads = [pick(grad_mixed[rows, window(pair)], mask) for mask in masks]
        weights = [probs[frame * HEADS + 2 * pair + index] for index in range(2)]
        value_part = nn(jnp.concatenate(weights, axis=1), jnp.concatenate(grads, axis=0))
        scores = []
        for weight, grad in zip(weights, grads):
            grad_attention = nt(values, grad)
            wide = weight.astype(F32)
            inner = jnp.sum(wide * grad_attention, axis=0, keepdims=True)
            scores.append((wide * (grad_attention - inner) * SCALE).astype(BF16))
        query_part = tn(
            jnp.concatenate(scores, axis=0),
            jnp.concatenate([pick(keys, mask) for mask in masks], axis=0),
        )
        key_part = nn(
            jnp.concatenate(scores, axis=1),
            jnp.concatenate([pick(queries, mask) for mask in masks], axis=0),
        )
        return (
            put(grad_packed, HALF, 0, pair, carries[0], query_part),
            put(grad_packed, HALF, D, pair, carries[1], key_part),
            put(grad_packed, HALF, 2 * D, pair, carries[2], value_part),
        )

    over_pairs(body, [(grad_packed, HALF, base) for base in (0, D, 2 * D)])


def own_keys(scores, lane_block):
    kept = pick(scores[:FRAMES], lane_block == 0)
    for block in range(1, 8):
        kept = jnp.where(
            lane_block == block, scores[FRAMES * block : FRAMES * (block + 1)], kept
        )
    return kept


def all_keys(kept, lane_block):
    return jnp.concatenate([pick(kept, lane_block == block) for block in range(8)], axis=0)


def temporal_pair(packed, grad_mixed, mixed, grad_packed, group):
    rows = slice(group * HW, group * HW + HW)

    def body(pair, carries):
        masks = pair_masks(pair)
        lane_block = lax.broadcasted_iota(jnp.int32, (1, 256), 1) // FRAMES
        queries = packed[HALF, window(pair)]
        keys = packed[HALF, window(pair, D)]
        values = packed[HALF, window(pair, 2 * D)]
        grads = [pick(grad_mixed[rows, window(pair)], mask) for mask in masks]
        own = [pick(keys, mask) for mask in masks]
        weights, scores = [], []
        for grad, key in zip(grads, own):
            weight = softmax_keys(own_keys(nt(key, queries), lane_block))
            grad_attention = own_keys(nt(values, grad), lane_block)
            inner = jnp.sum(weight * grad_attention, axis=0, keepdims=True)
            score = (weight * (grad_attention - inner) * SCALE).astype(BF16)
            weights.append(all_keys(weight.astype(BF16), lane_block))
            scores.append(all_keys(score, lane_block))
        mixed_part = tn(
            jnp.concatenate(weights, axis=0),
            jnp.concatenate([pick(values, mask) for mask in masks], axis=0),
        )
        value_part = nn(jnp.concatenate(weights, axis=1), jnp.concatenate(grads, axis=0))
        query_part = tn(jnp.concatenate(scores, axis=0), jnp.concatenate(own, axis=0))
        key_part = nn(
            jnp.concatenate(scores, axis=1),
            jnp.concatenate([pick(queries, mask) for mask in masks], axis=0),
        )
        return (
            put(mixed, rows, 0, pair, carries[0], mixed_part),
            put(grad_packed, HALF, 0, pair, carries[1], query_part),
            put(grad_packed, HALF, D, pair, carries[2], key_part),
            put(grad_packed, HALF, 2 * D, pair, carries[3], value_part),
        )

    over_pairs(
        body, [(mixed, rows, 0)] + [(grad_packed, HALF, base) for base in (0, D, 2 * D)]
    )


class Reduction:
    def __init__(self, part, first, summed, second, block, third, last, final, sems):
        self.part, self.first, self.summed, self.second = part, first, summed, second
        self.block, self.third, self.last, self.final = block, third, last, final
        self.first_send, self.first_recv, self.second_send, self.second_recv = sems[:4]
        self.third_send, self.third_recv, self.last_send, self.last_recv = sems[4:8]
        self.final_send, self.final_recv = sems[8:]
        self.me = lax.axis_index("seq")
        self.clip = lax.axis_index("dp")
        self.core = lax.rem(self.me, 2)
        self.chip = self.me // 2

    def to_core(self, index):
        return pltpu.make_async_remote_copy(
            src_ref=self.part.at[1 - self.core, index],
            dst_ref=self.first.at[index],
            send_sem=self.first_send.at[index],
            recv_sem=self.first_recv.at[index],
            device_id={"seq": self.me + 1 - 2 * self.core},
            device_id_type=MESH,
        )

    def to_chip(self, step):
        chip = lax.rem(self.chip + step, 8)
        return pltpu.make_async_remote_copy(
            src_ref=self.summed.at[chip],
            dst_ref=self.second.at[step],
            send_sem=self.second_send.at[step],
            recv_sem=self.second_recv.at[step],
            device_id={"seq": 2 * chip + self.core},
            device_id_type=MESH,
        )

    def to_clip(self, step, source):
        clip = lax.rem(self.clip + step, DP)
        return pltpu.make_async_remote_copy(
            src_ref=self.block.at[:, pl.ds(pl.multiple_of(128 * clip, 128), 128)],
            dst_ref=self.third.at[source],
            send_sem=self.third_send.at[step],
            recv_sem=self.third_recv.at[source],
            device_id={"dp": clip},
            device_id_type=MESH,
        )

    def to_clip_last(self, step, source):
        clip = lax.rem(self.clip + step, DP)
        return pltpu.make_async_remote_copy(
            src_ref=self.block.at[:, pl.ds(1024, 128)],
            dst_ref=self.last.at[source],
            send_sem=self.last_send.at[step],
            recv_sem=self.last_recv.at[source],
            device_id={"dp": clip},
            device_id_type=MESH,
        )

    def to_all(self, step, source):
        clip = lax.rem(self.clip + step, DP)
        columns = pl.ds(pl.multiple_of(128 * source, 128), 128)
        return pltpu.make_async_remote_copy(
            src_ref=self.final.at[:, columns],
            dst_ref=self.final.at[:, columns],
            send_sem=self.final_send.at[step],
            recv_sem=self.final_recv.at[source],
            device_id={"dp": clip},
            device_id_type=MESH,
        )

    def start(self, left, right):
        tail, at = None, 0
        for chunk in range(3):
            product = tn(left[:, 384 * chunk : 384 * chunk + 384], right[...])
            if tail is not None:
                product = jnp.concatenate([tail, product], axis=0)
            count = product.shape[0] // SHARE
            for index in range(count):
                share = product[SHARE * index : SHARE * index + SHARE]
                padding = jnp.zeros((PADDED - SHARE, D), F32)
                owner = at + index
                self.part[owner % 2, owner // 2] = jnp.concatenate(
                    [share, padding], axis=0
                ).astype(BF16)
            for index in range(at // 2, (at + count) // 2):
                self.to_core(index).start()
            at += count
            tail = product[SHARE * count :] if at < SEQ else None

    def over_cores(self):
        def send(step, carry):
            chip = lax.rem(self.chip + step, 8)
            self.to_core(chip).wait_recv()
            total = self.part[self.core, chip].astype(F32) + self.first[chip].astype(F32)
            self.summed[chip] = total.astype(BF16)

            @pl.when(step < 8)
            def _():
                self.to_chip(step).start()

            return carry

        lax.fori_loop(1, 9, send, 0)

    def over_seq(self):
        total = self.summed[self.chip].astype(F32)
        for step in range(1, 8):
            self.to_chip(step).wait_recv()
            total = total + self.second[step].astype(F32)
        self.block[...] = total.astype(BF16)
        self.third[self.clip] = self.block[:, pl.ds(pl.multiple_of(128 * self.clip, 128), 128)]
        self.last[self.clip] = self.block[:, 1024:1152]
        for step in range(1, DP):
            self.to_clip(step, self.clip).start()
            self.to_clip_last(step, self.clip).start()

    def over_clips(self):
        for step in range(1, DP):
            source = lax.rem(self.clip + step, DP)
            self.to_clip(step, source).wait_recv()
            self.to_clip_last(step, source).wait_recv()
        total, last = self.third[0].astype(F32), self.last[0].astype(F32)
        for source in range(1, DP):
            total = total + self.third[source].astype(F32)
            last = last + self.last[source].astype(F32)
        self.final[:, pl.ds(pl.multiple_of(128 * self.clip, 128), 128)] = total.astype(BF16)
        self.final[:, 1024:1152] = last.astype(BF16)
        for step in range(1, DP):
            self.to_all(step, self.clip).start()

    def finish(self, out, factor):
        for step in range(1, DP):
            self.to_all(step, lax.rem(self.clip + step, DP)).wait_recv()
        out[...] = self.final[:SHARE, :].astype(F32) * factor

    def drain(self):
        def cores(index, carry):
            self.to_core(index).wait_send()
            return carry

        def steps(step, carry):
            self.to_chip(step).wait_send()
            self.to_clip(step, self.clip).wait_send()
            self.to_clip_last(step, self.clip).wait_send()
            self.to_all(step, self.clip).wait_send()
            return carry

        lax.fori_loop(0, 8, cores, 0)
        lax.fori_loop(1, 8, steps, 0)


def kernel(
    x_hbm, cot_hbm, sqkv_hbm, sout_hbm, tqkv_hbm, tout_hbm,
    grad_hbm, sgrad, tgrad,
    x, cot, qkv, sout, tout,
    packed, mixed, probs, residual, residual_in, cot_in,
    res, cot_pos, packed_two, grad_mixed, mixed_two, grad_packed, grad_norm,
    back, back_in,
    t_part, t_first, t_summed, t_second, t_block, t_third, t_last, t_final,
    s_part, s_first, s_summed, s_second, s_block, s_third, s_last, s_final,
    load, swap, out_sem,
    cot_send, cot_recv, res_send, res_recv, back_send, back_recv,
    *sems,
):
    me, clip = lax.axis_index("seq"), lax.axis_index("dp")
    temporal_sum = Reduction(
        t_part, t_first, t_summed, t_second, t_block, t_third, t_last, t_final, sems[:10]
    )
    spatial_sum = Reduction(
        s_part, s_first, s_summed, s_second, s_block, s_third, s_last, s_final, sems[10:]
    )
    factor = 1.0 / math.sqrt(TOKENS * SEQ * DP)

    qkv_chunks = chunks(3 * D, 768)

    def load_qkv(source, index):
        at, size = qkv_chunks[index]
        columns = pl.ds(at, size)
        return pltpu.make_async_copy(source.at[:, columns], qkv.at[:, columns], swap.at[index])

    load_x = pltpu.make_async_copy(x_hbm, x, load.at[0])
    load_cot = pltpu.make_async_copy(cot_hbm, cot, load.at[1])
    load_sout = pltpu.make_async_copy(sout_hbm, sout, load.at[2])
    load_tout = pltpu.make_async_copy(tout_hbm, tout, load.at[3])
    load_x.start()
    for index in range(len(qkv_chunks)):
        load_qkv(sqkv_hbm, index).start()
    load_cot.start()
    load_sout.start()
    load_tout.start()

    barrier = pltpu.get_barrier_semaphore()

    def greet_seq(step, carry):
        pl.semaphore_signal(
            barrier, inc=1, device_id={"seq": lax.rem(me + step, SEQ)}, device_id_type=MESH
        )
        return carry

    def greet_dp(step, carry):
        pl.semaphore_signal(
            barrier, inc=1, device_id={"dp": lax.rem(clip + step, DP)}, device_id_type=MESH
        )
        return carry

    lax.fori_loop(1, SEQ, greet_seq, 0)
    lax.fori_loop(1, DP, greet_dp, 0)

    def send_cot(step):
        peer = lax.rem(me + step, SEQ)
        return pltpu.make_async_remote_copy(
            src_ref=cot.at[:, pl.ds(pl.multiple_of(16 * peer, 16), 16), :],
            dst_ref=cot_in.at[pl.ds(2 * me, 2)],
            send_sem=cot_send.at[step],
            recv_sem=cot_recv.at[step],
            device_id={"seq": peer},
            device_id_type=MESH,
        )

    def send_residual(step, frame):
        peer = lax.rem(me + step, SEQ)
        return pltpu.make_async_remote_copy(
            src_ref=residual.at[frame, pl.ds(pl.multiple_of(16 * peer, 16), 16), :],
            dst_ref=residual_in.at[2 * me + frame],
            send_sem=res_send.at[frame, step],
            recv_sem=res_recv.at[frame, step],
            device_id={"seq": peer},
            device_id_type=MESH,
        )

    def send_back(step, group):
        peer = lax.rem(me + step, SEQ)
        return pltpu.make_async_remote_copy(
            src_ref=back.at[peer, group],
            dst_ref=back_in.at[me, group],
            send_sem=back_send.at[group, step],
            recv_sem=back_recv.at[group, step],
            device_id={"seq": peer},
            device_id_type=MESH,
        )

    def each(action):
        def body(step, carry):
            action(step)
            return carry

        lax.fori_loop(1, SEQ, body, 0)

    load_x.wait()
    for frame in range(2):
        rows = slice(frame * HW, frame * HW + HW)
        norm, _ = rms_forward(x[frame])
        for index, (at, size) in enumerate(qkv_chunks):
            if frame == 0:
                load_qkv(sqkv_hbm, index).wait()
            packed[rows, at : at + size] = nn(norm, qkv[:, at : at + size]).astype(BF16)
        if frame == 0:
            load_cot.wait()
            pl.semaphore_wait(barrier, SEQ - 1 + DP - 1)
            each(lambda step: send_cot(step).start())
            cot_in[pl.ds(2 * me, 2)] = cot[:, pl.ds(pl.multiple_of(16 * me, 16), 16), :]
        else:
            for index in range(len(qkv_chunks)):
                load_qkv(tqkv_hbm, index).start()
        spatial_forward(packed, mixed, probs, frame)
        if frame == 0:
            load_sout.wait()
        for at, size in chunks(D, 256):
            residual[frame, :, at : at + size] = (
                x[frame, :, at : at + size].astype(F32) + nn(mixed[rows, :], sout[:, at : at + size])
            ).astype(BF16)
        each(lambda step: send_residual(step, frame).start())
        residual_in[2 * me + frame] = residual[frame, pl.ds(pl.multiple_of(16 * me, 16), 16), :]

    each(lambda step: send_cot(step).wait_recv())
    load_tout.wait()
    orders = [
        one_hot(
            HW, TOKENS, lambda row, group=group: (row % FRAMES) * 16 + group * 8 + row // FRAMES
        )
        for group in range(2)
    ]
    for group in range(2):
        rows = slice(group * HW, group * HW + HW)
        cot_pos[rows, :] = nn(orders[group], cot_in[...].reshape(TOKENS, D)).astype(BF16)
        for at, size in chunks(D, 256):
            grad_mixed[rows, at : at + size] = nt(cot_pos[rows, :], tout[at : at + size, :]).astype(
                BF16
            )

    for frame in range(2):
        each(lambda step: send_residual(step, frame).wait_recv())

    for group in range(2):
        rows = slice(group * HW, group * HW + HW)
        res[rows, :] = nn(orders[group], residual_in[...].reshape(TOKENS, D)).astype(BF16)
        norm, inverse = rms_forward(res[rows, :])
        for index, (at, size) in enumerate(qkv_chunks):
            if group == 0:
                load_qkv(tqkv_hbm, index).wait()
            packed_two[:, at : at + size] = nn(norm, qkv[:, at : at + size]).astype(BF16)
        temporal_pair(packed_two, grad_mixed, mixed_two, grad_packed, group)
        for at, size in chunks(D, 256):
            grad_norm[rows, at : at + size] = nt(grad_packed[...], qkv[at : at + size, :]).astype(
                BF16
            )
        if group == 1:
            for index in range(len(qkv_chunks)):
                load_qkv(sqkv_hbm, index).start()
        grad = (
            cot_pos[rows, :].astype(F32)
            + rms_backward(res[rows, :], grad_norm[rows, :], inverse)
        ).astype(BF16)
        order = one_hot(
            HW, HW, lambda row: (row % 8) * FRAMES + (row // 16) * 2 + (row // 8) % 2
        )
        back[:, group] = nn(order, grad).astype(BF16).reshape(SEQ, 16, D)
        each(lambda step: send_back(step, group).start())
        back_in[me, group] = back[me, group]

    temporal_sum.start(mixed_two, cot_pos)
    temporal_sum.over_cores()

    grad_res, grad_out = res, mixed_two
    for group in range(2):
        each(lambda step: send_back(step, group).wait_recv())
    for frame in range(2):
        rows = slice(frame * HW, frame * HW + HW)
        order = one_hot(HW, TOKENS, lambda row, frame=frame: (row // 8) * 16 + frame * 8 + row % 8)
        grad_res[rows, :] = nn(order, back_in[...].reshape(TOKENS, D)).astype(BF16)
    spatial_sum.start(mixed, grad_res)

    def store(frame):
        return pltpu.make_async_copy(
            grad_out.at[pl.ds(frame * HW, HW)], grad_hbm.at[frame], out_sem.at[frame]
        )

    for at, size in chunks(D, 256):
        grad_mixed[:, at : at + size] = nt(grad_res[...], sout[at : at + size, :]).astype(BF16)
    spatial_sum.over_cores()
    for index in range(len(qkv_chunks)):
        load_qkv(sqkv_hbm, index).wait()
    for frame in range(2):
        rows = slice(frame * HW, frame * HW + HW)
        spatial_backward(packed, grad_mixed, grad_packed, probs, frame)
        for at, size in chunks(D, 256):
            grad_norm[rows, at : at + size] = nt(grad_packed[...], qkv[at : at + size, :]).astype(
                BF16
            )
        _, inverse = rms_forward(x[frame])
        grad_out[rows, :] = (
            grad_res[rows, :].astype(F32) + rms_backward(x[frame], grad_norm[rows, :], inverse)
        ).astype(BF16)
        store(frame).start()
        if frame == 0:
            temporal_sum.over_seq()

    temporal_sum.over_clips()
    spatial_sum.over_seq()
    temporal_sum.finish(tgrad, factor)
    spatial_sum.over_clips()
    spatial_sum.finish(sgrad, factor)

    for frame in range(2):
        store(frame).wait()
        each(lambda step: send_residual(step, frame).wait_send())
        each(lambda step: send_back(step, frame).wait_send())
    each(lambda step: send_cot(step).wait_send())
    temporal_sum.drain()
    spatial_sum.drain()


def local(layer_input, cotangent, spatial_qkv, spatial_out, temporal_qkv, temporal_out):
    def vmem(*shape, dtype=BF16):
        return pltpu.VMEM(shape, dtype)

    reduction = [
        vmem(2, 8, PADDED, D),
        vmem(8, PADDED, D),
        vmem(8, PADDED, D),
        vmem(8, PADDED, D),
        vmem(PADDED, D),
        vmem(DP, PADDED, 128),
        vmem(DP, PADDED, 128),
        vmem(PADDED, D),
    ]
    dma = pltpu.SemaphoreType.DMA
    scratch = [
        vmem(2, HW, D), vmem(2, HW, D), vmem(D, 3 * D), vmem(D, D), vmem(D, D),
        vmem(TOKENS, 3 * D), vmem(TOKENS, D), vmem(2 * HEADS, HW, HW),
        vmem(2, HW, D), vmem(FRAMES, 16, D), vmem(FRAMES, 16, D),
        vmem(TOKENS, D), vmem(TOKENS, D), vmem(HW, 3 * D), vmem(TOKENS, D),
        vmem(TOKENS, D), vmem(HW, 3 * D), vmem(TOKENS, D),
        vmem(SEQ, 2, 16, D), vmem(SEQ, 2, 16, D),
        *reduction,
        *reduction,
        dma((4,)), dma((5,)), dma((2,)),
        dma((SEQ,)), dma((SEQ,)), dma((2, SEQ)), dma((2, SEQ)), dma((2, SEQ)), dma((2, SEQ)),
        *[dma((8,)) for _ in range(20)],
    ]
    hbm, on_chip = pl.BlockSpec(memory_space=pl.ANY), pl.BlockSpec(memory_space=pltpu.VMEM)
    grad, spatial_grad, temporal_grad = pl.pallas_call(
        kernel,
        out_shape=(
            jax.ShapeDtypeStruct((2, HW, D), BF16),
            jax.ShapeDtypeStruct((SHARE, D), F32),
            jax.ShapeDtypeStruct((SHARE, D), F32),
        ),
        in_specs=[hbm] * 6,
        out_specs=(hbm, on_chip, on_chip),
        scratch_shapes=scratch,
        compiler_params=pltpu.CompilerParams(
            collective_id=0, has_side_effects=True, vmem_limit_bytes=62 * 2**20
        ),
        cost_estimate=pl.CostEstimate(
            flops=40_000_000_000, bytes_accessed=40_000_000, transcendentals=3_000_000
        ),
        name="attention_pair_backward",
    )(
        layer_input.reshape(2, HW, D), cotangent.reshape(2, HW, D),
        spatial_qkv, spatial_out, temporal_qkv, temporal_out,
    )
    return grad.reshape(1, 2, HW, D), spatial_grad, temporal_grad


def solution(mesh):
    placed = (P("dp", "seq", None, None), P("dp", "seq", None, None), P(), P(), P(), P())
    return jax.shard_map(
        local,
        mesh=mesh,
        in_specs=placed,
        out_specs=(P("dp", "seq", None, None), P("seq", None), P("seq", None)),
        check_vma=False,
    )
```

```python
import functools
import math

import jax
import jax.numpy as jnp
from jax import lax
from jax.experimental import pallas as pl
from jax.experimental.pallas import tpu as pltpu
from jax.sharding import PartitionSpec as P

D = 1152
HEADS = 16
HEAD = D // HEADS
HW = 256
FRAMES = 32
SEQ = 16
DP = 8
TOKENS = 512
SHARE = D // SEQ
PADDED = 80
EPSILON = 1e-06
SCALE = 1.0 / math.sqrt(HEAD)
LOG2_E = math.log2(math.e)
F32 = jnp.float32
BF16 = jnp.bfloat16
MESH = pl.DeviceIdType.MESH
HALF = slice(0, HW)


def nn(left, right):
    return lax.dot_general(left, right, (((1,), (0,)), ((), ())), preferred_element_type=F32)


def nt(left, right):
    return lax.dot_general(left, right, (((1,), (1,)), ((), ())), preferred_element_type=F32)


def tn(left, right):
    return lax.dot_general(left, right, (((0,), (0,)), ((), ())), preferred_element_type=F32)


def chunks(width, step):
    return [(at, min(step, width - at)) for at in range(0, width, step)]


def rms_forward(block):
    widened = block.astype(F32)
    inverse = lax.rsqrt(jnp.mean(widened * widened, axis=-1, keepdims=True) + EPSILON)
    return (widened * inverse).astype(BF16), inverse


def rms_backward(block, grad_norm, inverse):
    widened = block.astype(F32)
    grad_wide = grad_norm.astype(F32)
    inner = jnp.mean(grad_wide * widened, axis=-1, keepdims=True)
    return inverse * grad_wide - widened * (inverse * inverse * inverse * inner)


def one_hot(rows, columns, target):
    row = lax.broadcasted_iota(jnp.int32, (rows, columns), 0)
    column = lax.broadcasted_iota(jnp.int32, (rows, columns), 1)
    return jnp.where(column == target(row), 1.0, 0.0).astype(BF16)


def pair_masks(pair):
    lane = lax.broadcasted_iota(jnp.int32, (1, 256), 1)
    first = (lane >= 16 * pair) & (lane < 16 * pair + HEAD)
    second = (lane >= 16 * pair + HEAD) & (lane < 16 * pair + 2 * HEAD)
    return first, second


def window(pair, base=0):
    return pl.ds(pl.multiple_of(128 * pair + base, 128), 256)


def tile(pair, base=0):
    return pl.ds(pl.multiple_of(128 * pair + base, 128), 128)


def pick(values, mask):
    return jnp.where(mask, values, jnp.zeros_like(values))


def put(ref, rows, base, pair, carry, result):
    ref[rows, tile(pair, base)] = (carry + result[:, :128]).astype(BF16)
    return result[:, 128:]


def softmax_keys(scores):
    top = jnp.max(scores, axis=0, keepdims=True)
    powers = jnp.exp2((scores - top) * (SCALE * LOG2_E))
    return powers * (1.0 / jnp.sum(powers, axis=0, keepdims=True))


def over_pairs(body, outputs):
    zero = jnp.zeros((HW, 128), F32)
    carries = lax.fori_loop(0, HEADS // 2, body, (zero,) * len(outputs), unroll=HEADS // 2)
    for (ref, rows, base), carry in zip(outputs, carries):
        ref[rows, base + 1024 : base + 1152] = carry.astype(BF16)


def spatial_forward(packed, mixed, probs, frame):
    rows = slice(frame * HW, frame * HW + HW)

    def body(pair, carries):
        masks = pair_masks(pair)
        queries = packed[rows, window(pair)]
        keys = packed[rows, window(pair, D)]
        values = packed[rows, window(pair, 2 * D)]
        weights = []
        for index, mask in enumerate(masks):
            weight = softmax_keys(nt(pick(keys, mask), queries)).astype(BF16)
            probs[frame * HEADS + 2 * pair + index] = weight
            weights.append(weight)
        result = tn(
            jnp.concatenate(weights, axis=0),
            jnp.concatenate([pick(values, mask) for mask in masks], axis=0),
        )
        return (put(mixed, rows, 0, pair, carries[0], result),)

    over_pairs(body, [(mixed, rows, 0)])


def spatial_backward(packed, grad_mixed, grad_packed, probs, frame):
    rows = slice(frame * HW, frame * HW + HW)

    def body(pair, carries):
        masks = pair_masks(pair)
        queries = packed[rows, window(pair)]
        keys = packed[rows, window(pair, D)]
        values = packed[rows, window(pair, 2 * D)]
        grads = [pick(grad_mixed[rows, window(pair)], mask) for mask in masks]
        weights = [probs[frame * HEADS + 2 * pair + index] for index in range(2)]
        value_part = nn(jnp.concatenate(weights, axis=1), jnp.concatenate(grads, axis=0))
        scores = []
        for weight, grad in zip(weights, grads):
            grad_attention = nt(values, grad)
            wide = weight.astype(F32)
            inner = jnp.sum(wide * grad_attention, axis=0, keepdims=True)
            scores.append((wide * (grad_attention - inner) * SCALE).astype(BF16))
        query_part = tn(
            jnp.concatenate(scores, axis=0),
            jnp.concatenate([pick(keys, mask) for mask in masks], axis=0),
        )
        key_part = nn(
            jnp.concatenate(scores, axis=1),
            jnp.concatenate([pick(queries, mask) for mask in masks], axis=0),
        )
        return (
            put(grad_packed, HALF, 0, pair, carries[0], query_part),
            put(grad_packed, HALF, D, pair, carries[1], key_part),
            put(grad_packed, HALF, 2 * D, pair, carries[2], value_part),
        )

    over_pairs(body, [(grad_packed, HALF, base) for base in (0, D, 2 * D)])


def own_keys(scores, lane_block):
    kept = pick(scores[:FRAMES], lane_block == 0)
    for block in range(1, 8):
        kept = jnp.where(
            lane_block == block, scores[FRAMES * block : FRAMES * (block + 1)], kept
        )
    return kept


def all_keys(kept, lane_block):
    return jnp.concatenate([pick(kept, lane_block == block) for block in range(8)], axis=0)


def temporal_forward(packed, mixed, probs, group):
    rows = slice(group * HW, group * HW + HW)

    def body(pair, carries):
        masks = pair_masks(pair)
        lane_block = lax.broadcasted_iota(jnp.int32, (1, 256), 1) // FRAMES
        queries = packed[rows, window(pair)]
        keys = packed[rows, window(pair, D)]
        values = packed[rows, window(pair, 2 * D)]
        weights = []
        for index, mask in enumerate(masks):
            weight = softmax_keys(own_keys(nt(pick(keys, mask), queries), lane_block)).astype(BF16)
            probs[group * HEADS + 2 * pair + index] = weight
            weights.append(all_keys(weight, lane_block))
        result = tn(
            jnp.concatenate(weights, axis=0),
            jnp.concatenate([pick(values, mask) for mask in masks], axis=0),
        )
        return (put(mixed, rows, 0, pair, carries[0], result),)

    over_pairs(body, [(mixed, rows, 0)])


def temporal_backward(packed, grad_mixed, grad_packed, probs, group):
    rows = slice(group * HW, group * HW + HW)

    def body(pair, carries):
        masks = pair_masks(pair)
        lane_block = lax.broadcasted_iota(jnp.int32, (1, 256), 1) // FRAMES
        queries = packed[rows, window(pair)]
        keys = packed[rows, window(pair, D)]
        values = packed[rows, window(pair, 2 * D)]
        grads = [pick(grad_mixed[rows, window(pair)], mask) for mask in masks]
        weights, scores = [], []
        for index, grad in enumerate(grads):
            weight = probs[group * HEADS + 2 * pair + index]
            grad_attention = own_keys(nt(values, grad), lane_block)
            wide = weight.astype(F32)
            inner = jnp.sum(wide * grad_attention, axis=0, keepdims=True)
            score = (wide * (grad_attention - inner) * SCALE).astype(BF16)
            weights.append(all_keys(weight, lane_block))
            scores.append(all_keys(score, lane_block))
        value_part = nn(jnp.concatenate(weights, axis=1), jnp.concatenate(grads, axis=0))
        query_part = tn(
            jnp.concatenate(scores, axis=0),
            jnp.concatenate([pick(keys, mask) for mask in masks], axis=0),
        )
        key_part = nn(
            jnp.concatenate(scores, axis=1),
            jnp.concatenate([pick(queries, mask) for mask in masks], axis=0),
        )
        return (
            put(grad_packed, HALF, 0, pair, carries[0], query_part),
            put(grad_packed, HALF, D, pair, carries[1], key_part),
            put(grad_packed, HALF, 2 * D, pair, carries[2], value_part),
        )

    over_pairs(body, [(grad_packed, HALF, base) for base in (0, D, 2 * D)])


def weight_shares(left, right, part, ready):
    tail, at = None, 0
    for chunk in range(3):
        product = tn(left[:, 384 * chunk : 384 * chunk + 384], right[...])
        if tail is not None:
            product = jnp.concatenate([tail, product], axis=0)
        count = product.shape[0] // SHARE
        for index in range(count):
            share = product[SHARE * index : SHARE * index + SHARE]
            padding = jnp.zeros((PADDED - SHARE, D), F32)
            core, chip = (at + index) % 2, (at + index) // 2
            part[core, chip // 4, chip % 4] = jnp.concatenate([share, padding], axis=0).astype(BF16)
        for chip in range(at // 2, (at + count) // 2):
            ready(chip)
        at += count
        tail = product[SHARE * count :] if at < SEQ else None


class Reduction:
    def __init__(self, part, first, sems):
        self.part, self.first = part, first
        self.first_send, self.first_recv = sems
        self.me = lax.axis_index("seq")
        self.clip = lax.axis_index("dp")
        self.core = lax.rem(self.me, 2)
        self.chip = self.me // 2
        self.along_x = lax.rem(self.clip, 4)
        self.along_y = self.clip // 4
        self.along_z = lax.rem(self.chip, 4)

    def copy(self, source, target, send, recv, device):
        return pltpu.make_async_remote_copy(
            src_ref=source,
            dst_ref=target,
            send_sem=send,
            recv_sem=recv,
            device_id=device,
            device_id_type=MESH,
        )

    def to_core(self, chip):
        return self.copy(
            self.part.at[1 - self.core, chip // 4, lax.rem(chip, 4)],
            self.first.at[chip // 4, lax.rem(chip, 4)],
            self.first_send.at[chip],
            self.first_recv.at[chip],
            {"seq": self.me + 1 - 2 * self.core},
        )

    def start(self, left, right):
        weight_shares(left, right, self.part, lambda chip: self.to_core(chip).start())

    def add_cores(self, chip):
        self.to_core(chip).wait_recv()
        high, low = chip // 4, lax.rem(chip, 4)
        total = self.part[self.core, high, low].astype(F32) + self.first[high, low].astype(F32)
        self.part[self.core, high, low] = total.astype(BF16)

    def drain_cores(self):
        def cores(chip, carry):
            self.to_core(chip).wait_send()
            return carry

        lax.fori_loop(0, 8, cores, 0)


class ClipsLast(Reduction):
    def __init__(self, part, first, second, block, third, last, final, sems):
        super().__init__(part, first, sems[:2])
        self.second, self.block, self.third = second, block, third
        self.last, self.final = last, final
        self.second_send, self.second_recv = sems[2:4]
        self.third_send, self.third_recv, self.last_send, self.last_recv = sems[4:8]
        self.final_send, self.final_recv = sems[8:]

    def to_chip(self, step):
        chip = lax.rem(self.chip + step, 8)
        return self.copy(
            self.part.at[self.core, chip // 4, lax.rem(chip, 4)],
            self.second.at[step],
            self.second_send.at[step],
            self.second_recv.at[step],
            {"seq": 2 * chip + self.core},
        )

    def to_clip(self, step, source):
        clip = lax.rem(self.clip + step, DP)
        return self.copy(
            self.block.at[:, pl.ds(pl.multiple_of(128 * clip, 128), 128)],
            self.third.at[source],
            self.third_send.at[step],
            self.third_recv.at[source],
            {"dp": clip},
        )

    def to_clip_last(self, step, source):
        return self.copy(
            self.block.at[:, pl.ds(1024, 128)],
            self.last.at[source],
            self.last_send.at[step],
            self.last_recv.at[source],
            {"dp": lax.rem(self.clip + step, DP)},
        )

    def to_all(self, step, source):
        columns = pl.ds(pl.multiple_of(128 * source, 128), 128)
        return self.copy(
            self.final.at[:, columns],
            self.final.at[:, columns],
            self.final_send.at[step],
            self.final_recv.at[source],
            {"dp": lax.rem(self.clip + step, DP)},
        )

    def over_cores(self):
        def send(step, carry):
            self.add_cores(lax.rem(self.chip + step, 8))

            @pl.when(step < 8)
            def _():
                self.to_chip(step).start()

            return carry

        lax.fori_loop(1, 9, send, 0)

    def over_seq(self):
        total = self.part[self.core, self.chip // 4, self.along_z].astype(F32)
        for step in range(1, 8):
            self.to_chip(step).wait_recv()
            total = total + self.second[step].astype(F32)
        self.block[...] = total.astype(BF16)
        self.third[self.clip] = self.block[:, pl.ds(pl.multiple_of(128 * self.clip, 128), 128)]
        self.last[self.clip] = self.block[:, 1024:1152]
        for step in range(1, DP):
            self.to_clip(step, self.clip).start()
            self.to_clip_last(step, self.clip).start()

    def over_clips(self):
        for step in range(1, DP):
            source = lax.rem(self.clip + step, DP)
            self.to_clip(step, source).wait_recv()
            self.to_clip_last(step, source).wait_recv()
        total, last = self.third[0].astype(F32), self.last[0].astype(F32)
        for source in range(1, DP):
            total = total + self.third[source].astype(F32)
            last = last + self.last[source].astype(F32)
        self.final[:, pl.ds(pl.multiple_of(128 * self.clip, 128), 128)] = total.astype(BF16)
        self.final[:, 1024:1152] = last.astype(BF16)
        for step in range(1, DP):
            self.to_all(step, self.clip).start()

    def finish(self, out, factor):
        for step in range(1, DP):
            self.to_all(step, lax.rem(self.clip + step, DP)).wait_recv()
        out[...] = self.final[:SHARE, :].astype(F32) * factor

    def drain(self):
        def steps(step, carry):
            self.to_chip(step).wait_send()
            self.to_clip(step, self.clip).wait_send()
            self.to_clip_last(step, self.clip).wait_send()
            self.to_all(step, self.clip).wait_send()
            return carry

        self.drain_cores()
        lax.fori_loop(1, 8, steps, 0)


class RowsFirst(Reduction):
    def __init__(self, part, first, wide, wide_last, second, second_last, final, sems):
        super().__init__(part, first, sems[:2])
        self.wide, self.wide_last = wide, wide_last
        self.second, self.second_last, self.final = second, second_last, final
        self.wide_send, self.wide_recv, self.wide_last_send, self.wide_last_recv = sems[2:6]
        self.second_send, self.second_recv = sems[6:8]
        self.second_last_send, self.second_last_recv = sems[8:10]
        self.final_send, self.final_recv, self.final_last_send, self.final_last_recv = sems[10:]

    def columns(self, along_x):
        return pl.ds(pl.multiple_of(256 * along_x, 256), 256)

    def to_x(self, step, source):
        along_x = lax.rem(self.along_x + step, 4)
        return self.copy(
            self.part.at[self.core, :, :, :, self.columns(along_x)],
            self.wide.at[source],
            self.wide_send.at[step],
            self.wide_recv.at[source],
            {"dp": 4 * self.along_y + along_x},
        )

    def to_x_last(self, step, source):
        along_x = lax.rem(self.along_x + step, 4)
        return self.copy(
            self.part.at[self.core, :, along_x, :, pl.ds(1024, 128)],
            self.wide_last.at[source],
            self.wide_last_send.at[step],
            self.wide_last_recv.at[source],
            {"dp": 4 * self.along_y + along_x},
        )

    def to_chip(self, step):
        chip = lax.rem(self.chip + step, 8)
        return self.copy(
            self.wide.at[self.along_x, chip // 4, lax.rem(chip, 4)],
            self.second.at[step],
            self.second_send.at[step],
            self.second_recv.at[step],
            {"seq": 2 * chip + self.core},
        )

    def to_chip_last(self, step):
        chip = lax.rem(self.chip + step, 8)
        return self.copy(
            self.wide_last.at[self.along_x, chip // 4],
            self.second_last.at[step],
            self.second_last_send.at[step],
            self.second_last_recv.at[step],
            {"seq": 2 * chip + self.core},
        )

    def to_all(self, step, source):
        place = self.final.at[source // 4, :, self.columns(lax.rem(source, 4))]
        return self.copy(
            place,
            place,
            self.final_send.at[step],
            self.final_recv.at[source],
            {"dp": lax.rem(self.clip + step, DP)},
        )

    def to_all_last(self, step, source):
        place = self.final.at[source // 4, :, pl.ds(1024, 128)]
        return self.copy(
            place,
            place,
            self.final_last_send.at[step],
            self.final_last_recv.at[source],
            {"dp": lax.rem(self.clip + step, DP)},
        )

    def over_cores(self):
        def add(chip, carry):
            self.add_cores(chip)
            return carry

        lax.fori_loop(0, 8, add, 0)
        for step in range(1, 4):
            self.to_x(step, self.along_x).start()
            self.to_x_last(step, self.along_x).start()

    def over_x(self):
        for step in range(1, 4):
            source = lax.rem(self.along_x + step, 4)
            self.to_x(step, source).wait_recv()
            self.to_x_last(step, source).wait_recv()
        for high in range(2):
            for low in range(4):
                total = self.part[self.core, high, low, :, self.columns(self.along_x)].astype(F32)
                for step in range(1, 4):
                    total = total + self.wide[lax.rem(self.along_x + step, 4), high, low].astype(F32)
                self.wide[self.along_x, high, low] = total.astype(BF16)
            total = self.part[self.core, high, self.along_x, :, 1024:1152].astype(F32)
            for step in range(1, 4):
                total = total + self.wide_last[lax.rem(self.along_x + step, 4), high].astype(F32)
            self.wide_last[self.along_x, high] = total.astype(BF16)

        def send(step, carry):
            self.to_chip(step).start()

            @pl.when(lax.rem(self.chip + step, 4) == self.along_x)
            def _():
                self.to_chip_last(step).start()

            return carry

        lax.fori_loop(1, 8, send, 0)

    def over_seq(self):
        high = self.chip // 4
        total = self.wide[self.along_x, high, self.along_z].astype(F32)
        for step in range(1, 8):
            self.to_chip(step).wait_recv()
            total = total + self.second[step].astype(F32)
        self.final[self.along_y, :, self.columns(self.along_x)] = total.astype(BF16)

        @pl.when(self.along_z == self.along_x)
        def _():
            last = self.wide_last[self.along_x, high].astype(F32)
            for step in range(1, 8):
                self.to_chip_last(step).wait_recv()
                last = last + self.second_last[step].astype(F32)
            self.final[self.along_y, :, 1024:1152] = last.astype(BF16)
            for step in range(1, DP):
                self.to_all_last(step, self.clip).start()

        for step in range(1, DP):
            self.to_all(step, self.clip).start()

    def finish(self, out, factor):
        for step in range(1, DP):
            source = lax.rem(self.clip + step, DP)
            self.to_all(step, source).wait_recv()

            @pl.when(lax.rem(source, 4) == self.along_z)
            def _():
                self.to_all_last(step, source).wait_recv()

        total = self.final[0, :SHARE, :].astype(F32) + self.final[1, :SHARE, :].astype(F32)
        out[...] = total * factor

    def drain(self):
        for step in range(1, 4):
            self.to_x(step, self.along_x).wait_send()
            self.to_x_last(step, self.along_x).wait_send()

        def steps(step, carry):
            self.to_chip(step).wait_send()
            self.to_all(step, self.clip).wait_send()

            @pl.when(lax.rem(self.chip + step, 4) == self.along_x)
            def _():
                self.to_chip_last(step).wait_send()

            @pl.when(self.along_z == self.along_x)
            def _():
                self.to_all_last(step, self.clip).wait_send()

            return carry

        self.drain_cores()
        lax.fori_loop(1, 8, steps, 0)


def kernel(
    x_hbm, cot_hbm, sqkv_hbm, sout_hbm, tqkv_hbm, tout_hbm,
    grad_hbm, sgrad, tgrad,
    x, cot, qkv, sout, tout,
    packed, mixed, probs, temporal_probs, residual, residual_in, cot_in,
    res, cot_pos, packed_two, grad_mixed, mixed_two, grad_packed, grad_norm,
    back, back_in,
    t_part, t_first, t_wide, t_wide_last, t_second, t_second_last, t_final,
    s_part, s_first, s_second, s_block, s_third, s_last, s_final,
    load, swap, out_sem,
    cot_send, cot_recv, res_send, res_recv, back_send, back_recv,
    *sems,
):
    me, clip = lax.axis_index("seq"), lax.axis_index("dp")
    temporal_sum = RowsFirst(
        t_part, t_first, t_wide, t_wide_last, t_second, t_second_last, t_final, sems[:14]
    )
    spatial_sum = ClipsLast(
        s_part, s_first, s_second, s_block, s_third, s_last, s_final, sems[14:]
    )
    factor = 1.0 / math.sqrt(TOKENS * SEQ * DP)

    qkv_chunks = chunks(3 * D, 768)

    def load_qkv(source, index):
        at, size = qkv_chunks[index]
        columns = pl.ds(at, size)
        return pltpu.make_async_copy(source.at[:, columns], qkv.at[:, columns], swap.at[index])

    load_x = pltpu.make_async_copy(x_hbm, x, load.at[0])
    load_cot = pltpu.make_async_copy(cot_hbm, cot, load.at[1])
    load_sout = pltpu.make_async_copy(sout_hbm, sout, load.at[2])
    load_tout = pltpu.make_async_copy(tout_hbm, tout, load.at[3])
    load_x.start()
    for index in range(len(qkv_chunks)):
        load_qkv(sqkv_hbm, index).start()
    load_cot.start()
    load_sout.start()
    load_tout.start()

    barrier = pltpu.get_barrier_semaphore()

    def greet_seq(step, carry):
        pl.semaphore_signal(
            barrier, inc=1, device_id={"seq": lax.rem(me + step, SEQ)}, device_id_type=MESH
        )
        return carry

    def greet_dp(step, carry):
        pl.semaphore_signal(
            barrier, inc=1, device_id={"dp": lax.rem(clip + step, DP)}, device_id_type=MESH
        )
        return carry

    lax.fori_loop(1, SEQ, greet_seq, 0)
    lax.fori_loop(1, DP, greet_dp, 0)

    def send_cot(step, frame):
        peer = lax.rem(me + step, SEQ)
        return pltpu.make_async_remote_copy(
            src_ref=cot.at[frame, pl.ds(pl.multiple_of(16 * peer, 16), 16), :],
            dst_ref=cot_in.at[2 * me + frame],
            send_sem=cot_send.at[frame, step],
            recv_sem=cot_recv.at[frame, step],
            device_id={"seq": peer},
            device_id_type=MESH,
        )

    def send_residual(step, frame):
        peer = lax.rem(me + step, SEQ)
        return pltpu.make_async_remote_copy(
            src_ref=residual.at[frame, pl.ds(pl.multiple_of(16 * peer, 16), 16), :],
            dst_ref=residual_in.at[2 * me + frame],
            send_sem=res_send.at[frame, step],
            recv_sem=res_recv.at[frame, step],
            device_id={"seq": peer},
            device_id_type=MESH,
        )

    def send_back(step, group):
        peer = lax.rem(me + step, SEQ)
        return pltpu.make_async_remote_copy(
            src_ref=back.at[peer, group],
            dst_ref=back_in.at[me, group],
            send_sem=back_send.at[group, step],
            recv_sem=back_recv.at[group, step],
            device_id={"seq": peer},
            device_id_type=MESH,
        )

    def each(action):
        def body(step, carry):
            action(step)
            return carry

        lax.fori_loop(1, SEQ, body, 0)

    load_x.wait()
    for frame in range(2):
        rows = slice(frame * HW, frame * HW + HW)
        norm, _ = rms_forward(x[frame])
        for index, (at, size) in enumerate(qkv_chunks):
            if frame == 0:
                load_qkv(sqkv_hbm, index).wait()
            packed[rows, at : at + size] = nn(norm, qkv[:, at : at + size]).astype(BF16)
        if frame == 0:
            load_cot.wait()
            pl.semaphore_wait(barrier, SEQ - 1 + DP - 1)
            each(lambda step: send_cot(step, 0).start())
            cot_in[pl.ds(2 * me, 2)] = cot[:, pl.ds(pl.multiple_of(16 * me, 16), 16), :]
        else:
            for index in range(len(qkv_chunks)):
                load_qkv(tqkv_hbm, index).start()
        spatial_forward(packed, mixed, probs, frame)
        if frame == 0:
            load_sout.wait()
        for at, size in chunks(D, 256):
            residual[frame, :, at : at + size] = (
                x[frame, :, at : at + size].astype(F32) + nn(mixed[rows, :], sout[:, at : at + size])
            ).astype(BF16)
        each(lambda step: send_residual(step, frame).start())
        residual_in[2 * me + frame] = residual[frame, pl.ds(pl.multiple_of(16 * me, 16), 16), :]

    each(lambda step: send_cot(step, 1).start())
    for frame in range(2):
        each(lambda step: send_residual(step, frame).wait_recv())

    orders = [
        one_hot(
            HW, TOKENS, lambda row, group=group: (row % FRAMES) * 16 + group * 8 + row // FRAMES
        )
        for group in range(2)
    ]
    inverses = []
    for group in range(2):
        rows = slice(group * HW, group * HW + HW)
        res[rows, :] = nn(orders[group], residual_in[...].reshape(TOKENS, D)).astype(BF16)
        norm, inverse = rms_forward(res[rows, :])
        inverses.append(inverse)
        for index, (at, size) in enumerate(qkv_chunks):
            if group == 0:
                load_qkv(tqkv_hbm, index).wait()
            packed_two[rows, at : at + size] = nn(norm, qkv[:, at : at + size]).astype(BF16)
        temporal_forward(packed_two, mixed_two, temporal_probs, group)

    load_tout.wait()
    for frame in range(2):
        each(lambda step: send_cot(step, frame).wait_recv())
    for group in range(2):
        rows = slice(group * HW, group * HW + HW)
        cot_pos[rows, :] = nn(orders[group], cot_in[...].reshape(TOKENS, D)).astype(BF16)
        for at, size in chunks(D, 256):
            grad_mixed[rows, at : at + size] = nt(cot_pos[rows, :], tout[at : at + size, :]).astype(
                BF16
            )
        temporal_backward(packed_two, grad_mixed, grad_packed, temporal_probs, group)
        for at, size in chunks(D, 256):
            grad_norm[rows, at : at + size] = nt(grad_packed[...], qkv[at : at + size, :]).astype(
                BF16
            )
        if group == 1:
            for index in range(len(qkv_chunks)):
                load_qkv(sqkv_hbm, index).start()
        grad = (
            cot_pos[rows, :].astype(F32)
            + rms_backward(res[rows, :], grad_norm[rows, :], inverses[group])
        ).astype(BF16)
        order = one_hot(
            HW, HW, lambda row: (row % 8) * FRAMES + (row // 16) * 2 + (row // 8) % 2
        )
        back[:, group] = nn(order, grad).astype(BF16).reshape(SEQ, 16, D)
        each(lambda step: send_back(step, group).start())
        back_in[me, group] = back[me, group]

    temporal_sum.start(mixed_two, cot_pos)
    temporal_sum.over_cores()

    grad_res, grad_out = res, mixed_two
    for group in range(2):
        each(lambda step: send_back(step, group).wait_recv())
    for frame in range(2):
        rows = slice(frame * HW, frame * HW + HW)
        order = one_hot(HW, TOKENS, lambda row, frame=frame: (row // 8) * 16 + frame * 8 + row % 8)
        grad_res[rows, :] = nn(order, back_in[...].reshape(TOKENS, D)).astype(BF16)
    spatial_sum.start(mixed, grad_res)

    def store(frame):
        return pltpu.make_async_copy(
            grad_out.at[pl.ds(frame * HW, HW)], grad_hbm.at[frame], out_sem.at[frame]
        )

    for at, size in chunks(D, 256):
        grad_mixed[:, at : at + size] = nt(grad_res[...], sout[at : at + size, :]).astype(BF16)
    spatial_sum.over_cores()
    for index in range(len(qkv_chunks)):
        load_qkv(sqkv_hbm, index).wait()
    for frame in range(2):
        rows = slice(frame * HW, frame * HW + HW)
        spatial_backward(packed, grad_mixed, grad_packed, probs, frame)
        for at, size in chunks(D, 256):
            grad_norm[rows, at : at + size] = nt(grad_packed[...], qkv[at : at + size, :]).astype(
                BF16
            )
        _, inverse = rms_forward(x[frame])
        grad_out[rows, :] = (
            grad_res[rows, :].astype(F32) + rms_backward(x[frame], grad_norm[rows, :], inverse)
        ).astype(BF16)
        store(frame).start()
        if frame == 0:
            temporal_sum.over_x()

    temporal_sum.over_seq()
    spatial_sum.over_seq()
    temporal_sum.finish(tgrad, factor)
    spatial_sum.over_clips()
    spatial_sum.finish(sgrad, factor)

    for frame in range(2):
        store(frame).wait()
        each(lambda step: send_residual(step, frame).wait_send())
        each(lambda step: send_back(step, frame).wait_send())
        each(lambda step: send_cot(step, frame).wait_send())
    temporal_sum.drain()
    spatial_sum.drain()


def local(layer_input, cotangent, spatial_qkv, spatial_out, temporal_qkv, temporal_out):
    def vmem(*shape, dtype=BF16):
        return pltpu.VMEM(shape, dtype)

    by_rows = [
        vmem(2, 2, 4, PADDED, D), vmem(2, 4, PADDED, D),
        vmem(4, 2, 4, PADDED, 256), vmem(4, 2, PADDED, 128),
        vmem(8, PADDED, 256), vmem(8, PADDED, 128), vmem(2, PADDED, D),
    ]
    by_clips = [
        vmem(2, 2, 4, PADDED, D), vmem(2, 4, PADDED, D), vmem(8, PADDED, D), vmem(PADDED, D),
        vmem(DP, PADDED, 128), vmem(DP, PADDED, 128), vmem(PADDED, D),
    ]
    dma = pltpu.SemaphoreType.DMA
    scratch = [
        vmem(2, HW, D), vmem(2, HW, D), vmem(D, 3 * D), vmem(D, D), vmem(D, D),
        vmem(TOKENS, 3 * D), vmem(TOKENS, D), vmem(2 * HEADS, HW, HW), vmem(2 * HEADS, FRAMES, HW),
        vmem(2, HW, D), vmem(FRAMES, 16, D), vmem(FRAMES, 16, D),
        vmem(TOKENS, D), vmem(TOKENS, D), vmem(TOKENS, 3 * D), vmem(TOKENS, D),
        vmem(TOKENS, D), vmem(HW, 3 * D), vmem(TOKENS, D),
        vmem(SEQ, 2, 16, D), vmem(SEQ, 2, 16, D),
        *by_rows,
        *by_clips,
        dma((4,)), dma((5,)), dma((2,)),
        dma((2, SEQ)), dma((2, SEQ)), dma((2, SEQ)), dma((2, SEQ)), dma((2, SEQ)), dma((2, SEQ)),
        *[dma((8,)) for _ in range(24)],
    ]
    hbm, on_chip = pl.BlockSpec(memory_space=pl.ANY), pl.BlockSpec(memory_space=pltpu.VMEM)
    grad, spatial_grad, temporal_grad = pl.pallas_call(
        kernel,
        out_shape=(
            jax.ShapeDtypeStruct((2, HW, D), BF16),
            jax.ShapeDtypeStruct((SHARE, D), F32),
            jax.ShapeDtypeStruct((SHARE, D), F32),
        ),
        in_specs=[hbm] * 6,
        out_specs=(hbm, on_chip, on_chip),
        scratch_shapes=scratch,
        compiler_params=pltpu.CompilerParams(
            collective_id=0, has_side_effects=True, vmem_limit_bytes=62 * 2**20
        ),
        cost_estimate=pl.CostEstimate(
            flops=40_000_000_000, bytes_accessed=40_000_000, transcendentals=3_000_000
        ),
        name="attention_pair_backward",
    )(
        layer_input.reshape(2, HW, D), cotangent.reshape(2, HW, D),
        spatial_qkv, spatial_out, temporal_qkv, temporal_out,
    )
    return grad.reshape(1, 2, HW, D), spatial_grad, temporal_grad


def solution(mesh):
    placed = (P("dp", "seq", None, None), P("dp", "seq", None, None), P(), P(), P(), P())
    return jax.shard_map(
        local,
        mesh=mesh,
        in_specs=placed,
        out_specs=(P("dp", "seq", None, None), P("seq", None), P("seq", None)),
        check_vma=False,
    )
```

```python
import functools
import math

import jax
import jax.numpy as jnp
from jax import lax
from jax.experimental import pallas as pl
from jax.experimental.pallas import tpu as pltpu
from jax.sharding import PartitionSpec as P

D = 1152
HEADS = 16
HEAD = D // HEADS
HW = 256
FRAMES = 32
SEQ = 16
DP = 8
TOKENS = 512
SHARE = D // SEQ
PADDED = 80
EPSILON = 1e-06
SCALE = 1.0 / math.sqrt(HEAD)
LOG2_E = math.log2(math.e)
F32 = jnp.float32
BF16 = jnp.bfloat16
MESH = pl.DeviceIdType.MESH
HALF = slice(0, HW)


def nn(left, right):
    return lax.dot_general(left, right, (((1,), (0,)), ((), ())), preferred_element_type=F32)


def nt(left, right):
    return lax.dot_general(left, right, (((1,), (1,)), ((), ())), preferred_element_type=F32)


def tn(left, right):
    return lax.dot_general(left, right, (((0,), (0,)), ((), ())), preferred_element_type=F32)


def chunks(width, step):
    return [(at, min(step, width - at)) for at in range(0, width, step)]


def rms_forward(block):
    widened = block.astype(F32)
    inverse = lax.rsqrt(jnp.mean(widened * widened, axis=-1, keepdims=True) + EPSILON)
    return (widened * inverse).astype(BF16), inverse


def rms_backward(block, grad_norm, inverse):
    widened = block.astype(F32)
    grad_wide = grad_norm.astype(F32)
    inner = jnp.mean(grad_wide * widened, axis=-1, keepdims=True)
    return inverse * grad_wide - widened * (inverse * inverse * inverse * inner)


def one_hot(rows, columns, target):
    row = lax.broadcasted_iota(jnp.int32, (rows, columns), 0)
    column = lax.broadcasted_iota(jnp.int32, (rows, columns), 1)
    return jnp.where(column == target(row), 1.0, 0.0).astype(BF16)


def pair_masks(pair):
    lane = lax.broadcasted_iota(jnp.int32, (1, 256), 1)
    first = (lane >= 16 * pair) & (lane < 16 * pair + HEAD)
    second = (lane >= 16 * pair + HEAD) & (lane < 16 * pair + 2 * HEAD)
    return first, second


def window(pair, base=0):
    return pl.ds(pl.multiple_of(128 * pair + base, 128), 256)


def tile(pair, base=0):
    return pl.ds(pl.multiple_of(128 * pair + base, 128), 128)


def pick(values, mask):
    return jnp.where(mask, values, jnp.zeros_like(values))


def put(ref, rows, base, pair, carry, result):
    ref[rows, tile(pair, base)] = (carry + result[:, :128]).astype(BF16)
    return result[:, 128:]


def softmax_keys(scores):
    top = jnp.max(scores, axis=0, keepdims=True)
    powers = jnp.exp2((scores - top) * (SCALE * LOG2_E))
    return powers * (1.0 / jnp.sum(powers, axis=0, keepdims=True))


def over_pairs(body, outputs):
    zero = jnp.zeros((HW, 128), F32)
    carries = lax.fori_loop(0, HEADS // 2, body, (zero,) * len(outputs), unroll=HEADS // 2)
    for (ref, rows, base), carry in zip(outputs, carries):
        ref[rows, base + 1024 : base + 1152] = carry.astype(BF16)


def spatial_forward(packed, mixed, probs, frame):
    rows = slice(frame * HW, frame * HW + HW)

    def body(pair, carries):
        masks = pair_masks(pair)
        queries = packed[rows, window(pair)]
        keys = packed[rows, window(pair, D)]
        values = packed[rows, window(pair, 2 * D)]
        weights = []
        for index, mask in enumerate(masks):
            weight = softmax_keys(nt(pick(keys, mask), queries)).astype(BF16)
            probs[frame * HEADS + 2 * pair + index] = weight
            weights.append(weight)
        result = tn(
            jnp.concatenate(weights, axis=0),
            jnp.concatenate([pick(values, mask) for mask in masks], axis=0),
        )
        return (put(mixed, rows, 0, pair, carries[0], result),)

    over_pairs(body, [(mixed, rows, 0)])


def spatial_backward(packed, grad_mixed, grad_packed, probs, frame):
    rows = slice(frame * HW, frame * HW + HW)

    def body(pair, carries):
        masks = pair_masks(pair)
        queries = packed[rows, window(pair)]
        keys = packed[rows, window(pair, D)]
        values = packed[rows, window(pair, 2 * D)]
        grads = [pick(grad_mixed[rows, window(pair)], mask) for mask in masks]
        weights = [probs[frame * HEADS + 2 * pair + index] for index in range(2)]
        value_part = nn(jnp.concatenate(weights, axis=1), jnp.concatenate(grads, axis=0))
        scores = []
        for weight, grad in zip(weights, grads):
            grad_attention = nt(values, grad)
            wide = weight.astype(F32)
            inner = jnp.sum(wide * grad_attention, axis=0, keepdims=True)
            scores.append((wide * (grad_attention - inner) * SCALE).astype(BF16))
        query_part = tn(
            jnp.concatenate(scores, axis=0),
            jnp.concatenate([pick(keys, mask) for mask in masks], axis=0),
        )
        key_part = nn(
            jnp.concatenate(scores, axis=1),
            jnp.concatenate([pick(queries, mask) for mask in masks], axis=0),
        )
        return (
            put(grad_packed, HALF, 0, pair, carries[0], query_part),
            put(grad_packed, HALF, D, pair, carries[1], key_part),
            put(grad_packed, HALF, 2 * D, pair, carries[2], value_part),
        )

    over_pairs(body, [(grad_packed, HALF, base) for base in (0, D, 2 * D)])


def own_keys(scores, lane_block):
    kept = pick(scores[:FRAMES], lane_block == 0)
    for block in range(1, 8):
        kept = jnp.where(
            lane_block == block, scores[FRAMES * block : FRAMES * (block + 1)], kept
        )
    return kept


def all_keys(kept, lane_block):
    return jnp.concatenate([pick(kept, lane_block == block) for block in range(8)], axis=0)


def temporal_forward(packed, mixed, probs, group):
    rows = slice(group * HW, group * HW + HW)

    def body(pair, carries):
        masks = pair_masks(pair)
        lane_block = lax.broadcasted_iota(jnp.int32, (1, 256), 1) // FRAMES
        queries = packed[rows, window(pair)]
        keys = packed[rows, window(pair, D)]
        values = packed[rows, window(pair, 2 * D)]
        weights = []
        for index, mask in enumerate(masks):
            weight = softmax_keys(own_keys(nt(pick(keys, mask), queries), lane_block)).astype(BF16)
            probs[group * HEADS + 2 * pair + index] = weight
            weights.append(all_keys(weight, lane_block))
        result = tn(
            jnp.concatenate(weights, axis=0),
            jnp.concatenate([pick(values, mask) for mask in masks], axis=0),
        )
        return (put(mixed, rows, 0, pair, carries[0], result),)

    over_pairs(body, [(mixed, rows, 0)])


def temporal_backward(packed, grad_mixed, grad_packed, probs, group):
    rows = slice(group * HW, group * HW + HW)

    def body(pair, carries):
        masks = pair_masks(pair)
        lane_block = lax.broadcasted_iota(jnp.int32, (1, 256), 1) // FRAMES
        queries = packed[rows, window(pair)]
        keys = packed[rows, window(pair, D)]
        values = packed[rows, window(pair, 2 * D)]
        grads = [pick(grad_mixed[rows, window(pair)], mask) for mask in masks]
        weights, scores = [], []
        for index, grad in enumerate(grads):
            weight = probs[group * HEADS + 2 * pair + index]
            grad_attention = own_keys(nt(values, grad), lane_block)
            wide = weight.astype(F32)
            inner = jnp.sum(wide * grad_attention, axis=0, keepdims=True)
            score = (wide * (grad_attention - inner) * SCALE).astype(BF16)
            weights.append(all_keys(weight, lane_block))
            scores.append(all_keys(score, lane_block))
        value_part = nn(jnp.concatenate(weights, axis=1), jnp.concatenate(grads, axis=0))
        query_part = tn(
            jnp.concatenate(scores, axis=0),
            jnp.concatenate([pick(keys, mask) for mask in masks], axis=0),
        )
        key_part = nn(
            jnp.concatenate(scores, axis=1),
            jnp.concatenate([pick(queries, mask) for mask in masks], axis=0),
        )
        return (
            put(grad_packed, HALF, 0, pair, carries[0], query_part),
            put(grad_packed, HALF, D, pair, carries[1], key_part),
            put(grad_packed, HALF, 2 * D, pair, carries[2], value_part),
        )

    over_pairs(body, [(grad_packed, HALF, base) for base in (0, D, 2 * D)])


def weight_shares(left, right, part, ready):
    tail, at = None, 0
    for chunk in range(3):
        product = tn(left[:, 384 * chunk : 384 * chunk + 384], right[...])
        if tail is not None:
            product = jnp.concatenate([tail, product], axis=0)
        count = product.shape[0] // SHARE
        for index in range(count):
            share = product[SHARE * index : SHARE * index + SHARE]
            padding = jnp.zeros((PADDED - SHARE, D), F32)
            core, chip = (at + index) % 2, (at + index) // 2
            part[core, chip // 4, chip % 4] = jnp.concatenate([share, padding], axis=0).astype(BF16)
        for chip in range(at // 2, (at + count) // 2):
            ready(chip)
        at += count
        tail = product[SHARE * count :] if at < SEQ else None


def settle(ref, sem):
    pltpu.make_async_copy(ref, ref, sem).wait()


class Reduction:
    def __init__(self, part, first, sems):
        self.part, self.first = part, first
        self.first_send, self.first_recv = sems
        self.me = lax.axis_index("seq")
        self.clip = lax.axis_index("dp")
        self.core = lax.rem(self.me, 2)
        self.chip = self.me // 2
        self.along_x = lax.rem(self.clip, 4)
        self.along_y = self.clip // 4
        self.along_z = lax.rem(self.chip, 4)

    def copy(self, source, target, send, recv, device):
        return pltpu.make_async_remote_copy(
            src_ref=source,
            dst_ref=target,
            send_sem=send,
            recv_sem=recv,
            device_id=device,
            device_id_type=MESH,
        )

    def x_peer(self, step):
        return lax.rem(self.along_x + step, 4)

    def to_x(self, step, source, target, sems):
        device = {"dp": 4 * self.along_y + self.x_peer(step)}
        self.copy(source, target, sems.at[0], sems.at[1], device).start()

    def to_seq(self, step, source, target, sems):
        device = {"seq": 2 * lax.rem(self.chip + step, 8) + self.core}
        self.copy(source, target, sems.at[0], sems.at[1], device).start()

    def to_dp(self, step, place, sems):
        device = {"dp": lax.rem(self.clip + step, DP)}
        self.copy(place, place, sems.at[0], sems.at[1], device).start()

    def to_core(self, chip):
        return self.copy(
            self.part.at[1 - self.core, chip // 4, lax.rem(chip, 4)],
            self.first.at[chip // 4, lax.rem(chip, 4)],
            self.first_send,
            self.first_recv.at[chip],
            {"seq": self.me + 1 - 2 * self.core},
        )

    def start(self, left, right):
        weight_shares(left, right, self.part, lambda chip: self.to_core(chip).start())

    def add_cores(self, chip):
        self.to_core(chip).wait_recv()
        high, low = chip // 4, lax.rem(chip, 4)
        total = self.part[self.core, high, low].astype(F32) + self.first[high, low].astype(F32)
        self.part[self.core, high, low] = total.astype(BF16)

    def lanes(self, at, width):
        return pl.ds(pl.multiple_of(at, 128), width)

    def finish(self, out, factor):
        self.settle_all()
        total = self.final[0, :SHARE, :].astype(F32) + self.final[1, :SHARE, :].astype(F32)
        out[...] = total * factor


class TwoWays(Reduction):
    def __init__(self, part, first, wide, second, rest, block, third, last, final, sems, pairs):
        super().__init__(part, first, sems)
        self.wide, self.second, self.rest = wide, second, rest
        self.block, self.third, self.last, self.final = block, third, last, final
        (self.wide_sems, self.second_sems, self.rest_sems, self.third_sems, self.last_sems,
         self.final_sems, self.end_sems) = pairs

    def over_cores(self):
        def send(step, carry):
            chip = lax.rem(self.chip + step, 8)
            self.add_cores(chip)

            @pl.when(step < 8)
            def _():
                source = self.part.at[self.core, chip // 4, lax.rem(chip, 4), :, pl.ds(512, 640)]
                self.to_seq(step, source, self.rest.at[step], self.rest_sems)

            return carry

        lax.fori_loop(1, 9, send, 0)
        for step in range(1, 4):
            columns = self.lanes(128 * self.x_peer(step), 128)
            source = self.part.at[self.core, :, :, :, columns]
            self.to_x(step, source, self.wide.at[self.along_x], self.wide_sems)

    def second_stage(self):
        settle(self.wide.at[pl.ds(0, 3)], self.wide_sems.at[1])
        columns = self.lanes(128 * self.along_x, 128)
        total = self.part[self.core, :, :, :, columns].astype(F32)
        for step in range(1, 4):
            total = total + self.wide[self.x_peer(step)].astype(F32)
        self.wide[self.along_x] = total.astype(BF16)

        def send(step, carry):
            chip = lax.rem(self.chip + step, 8)
            source = self.wide.at[self.along_x, chip // 4, lax.rem(chip, 4)]
            self.to_seq(step, source, self.second.at[step], self.second_sems)
            return carry

        lax.fori_loop(1, 8, send, 0)
        settle(self.rest.at[pl.ds(1, 7)], self.rest_sems.at[1])
        total = self.part[self.core, self.chip // 4, self.along_z, :, 512:1152].astype(F32)
        for step in range(1, 8):
            total = total + self.rest[step].astype(F32)
        self.block[...] = total.astype(BF16)
        self.third[self.along_x] = self.block[:, columns]
        self.last[self.along_x] = self.block[:, 512:640]
        for step in range(1, 4):
            source = self.block.at[:, self.lanes(128 * self.x_peer(step), 128)]
            self.to_x(step, source, self.third.at[self.along_x], self.third_sems)
            source = self.block.at[:, pl.ds(512, 128)]
            self.to_x(step, source, self.last.at[self.along_x], self.last_sems)

    def third_stage(self):
        first, other = self.lanes(128 * self.along_x, 128), self.lanes(512 + 128 * self.along_x, 128)
        settle(self.second.at[pl.ds(1, 7)], self.second_sems.at[1])
        total = self.wide[self.along_x, self.chip // 4, self.along_z].astype(F32)
        for step in range(1, 8):
            total = total + self.second[step].astype(F32)
        self.final[self.along_y, :, first] = total.astype(BF16)
        for step in range(1, DP):
            self.to_dp(step, self.final.at[self.along_y, :, first], self.final_sems)
        settle(self.third.at[pl.ds(0, 3)], self.third_sems.at[1])
        settle(self.last.at[pl.ds(0, 3)], self.last_sems.at[1])
        total, last = self.third[0].astype(F32), self.last[0].astype(F32)
        for source in range(1, 4):
            total = total + self.third[source].astype(F32)
            last = last + self.last[source].astype(F32)
        self.final[self.along_y, :, other] = total.astype(BF16)
        self.final[self.along_y, :, 1024:1152] = last.astype(BF16)
        for step in range(1, DP):
            self.to_dp(step, self.final.at[self.along_y, :, other], self.final_sems)
        self.to_dp(4, self.final.at[self.along_y, :, pl.ds(1024, 128)], self.end_sems)

    def settle_all(self):
        settle(self.rest.at[pl.ds(0, 7), :, pl.ds(0, 256)], self.final_sems.at[1])
        settle(self.second.at[0], self.end_sems.at[1])

    def drain(self):
        settle(self.first, self.first_send)
        settle(self.rest.at[pl.ds(1, 7)], self.rest_sems.at[0])
        settle(self.wide.at[pl.ds(0, 3)], self.wide_sems.at[0])
        settle(self.second.at[pl.ds(1, 7)], self.second_sems.at[0])
        settle(self.third.at[pl.ds(0, 3)], self.third_sems.at[0])
        settle(self.last.at[pl.ds(0, 3)], self.last_sems.at[0])
        settle(self.rest.at[pl.ds(0, 7), :, pl.ds(0, 256)], self.final_sems.at[0])
        settle(self.second.at[0], self.end_sems.at[0])


class RowsFirst(Reduction):
    def __init__(self, part, first, wide, wide_last, second, second_last, final, sems, pairs):
        super().__init__(part, first, sems)
        self.wide, self.wide_last = wide, wide_last
        self.second, self.second_last, self.final = second, second_last, final
        (self.wide_sems, self.wide_last_sems, self.second_sems, self.second_last_sems,
         self.final_sems, self.final_last_sems) = pairs

    def over_cores(self):
        def add(chip, carry):
            self.add_cores(chip)
            return carry

        lax.fori_loop(0, 8, add, 0)
        for step in range(1, 4):
            peer = self.x_peer(step)
            source = self.part.at[self.core, :, :, :, self.lanes(256 * peer, 256)]
            self.to_x(step, source, self.wide.at[self.along_x], self.wide_sems)
            source = self.part.at[self.core, :, peer, :, pl.ds(1024, 128)]
            self.to_x(step, source, self.wide_last.at[self.along_x], self.wide_last_sems)

    def with_last(self, step):
        return lax.rem(self.chip + step, 4) == self.along_x

    def over_x(self):
        settle(self.wide.at[pl.ds(0, 3)], self.wide_sems.at[1])
        settle(self.wide_last.at[pl.ds(0, 3)], self.wide_last_sems.at[1])
        for high in range(2):
            columns = self.lanes(256 * self.along_x, 256)
            total = self.part[self.core, high, :, :, columns].astype(F32)
            last = self.part[self.core, high, self.along_x, :, 1024:1152].astype(F32)
            for step in range(1, 4):
                total = total + self.wide[self.x_peer(step), high].astype(F32)
                last = last + self.wide_last[self.x_peer(step), high].astype(F32)
            self.wide[self.along_x, high] = total.astype(BF16)
            self.wide_last[self.along_x, high] = last.astype(BF16)

        def send(step, carry):
            chip = lax.rem(self.chip + step, 8)
            source = self.wide.at[self.along_x, chip // 4, lax.rem(chip, 4)]
            self.to_seq(step, source, self.second.at[step], self.second_sems)

            @pl.when(self.with_last(step))
            def _():
                source = self.wide_last.at[self.along_x, chip // 4]
                self.to_seq(step, source, self.second_last.at[step], self.second_last_sems)

            return carry

        lax.fori_loop(1, 8, send, 0)

    def over_seq(self):
        high = self.chip // 4
        columns = self.lanes(256 * self.along_x, 256)
        settle(self.second.at[pl.ds(1, 7)], self.second_sems.at[1])
        total = self.wide[self.along_x, high, self.along_z].astype(F32)
        for step in range(1, 8):
            total = total + self.second[step].astype(F32)
        self.final[self.along_y, :, columns] = total.astype(BF16)
        for step in range(1, DP):
            self.to_dp(step, self.final.at[self.along_y, :, columns], self.final_sems)

        @pl.when(self.along_z == self.along_x)
        def _():
            settle(self.second_last.at[pl.ds(1, 7)], self.second_last_sems.at[1])
            last = self.wide_last[self.along_x, high].astype(F32)
            for step in range(1, 8):
                last = last + self.second_last[step].astype(F32)
            self.final[self.along_y, :, 1024:1152] = last.astype(BF16)
            for step in range(1, DP):
                place = self.final.at[self.along_y, :, pl.ds(1024, 128)]
                self.to_dp(step, place, self.final_last_sems)

    def settle_all(self):
        settle(self.second.at[pl.ds(0, 7)], self.final_sems.at[1])

        @pl.when(self.along_z == self.along_x)
        def _():
            settle(self.second_last.at[0], self.final_last_sems.at[1])

        @pl.when(self.along_z != self.along_x)
        def _():
            settle(self.second_last.at[pl.ds(0, 2)], self.final_last_sems.at[1])

    def drain(self):
        settle(self.first, self.first_send)
        settle(self.wide.at[pl.ds(0, 3)], self.wide_sems.at[0])
        settle(self.wide_last.at[pl.ds(0, 3)], self.wide_last_sems.at[0])
        settle(self.second.at[pl.ds(1, 7)], self.second_sems.at[0])
        settle(self.second.at[pl.ds(0, 7)], self.final_sems.at[0])

        @pl.when(self.along_z == self.along_x)
        def _():
            settle(self.second_last.at[0], self.second_last_sems.at[0])
            settle(self.second_last.at[pl.ds(0, 7)], self.final_last_sems.at[0])

        @pl.when(self.along_z != self.along_x)
        def _():
            settle(self.second_last.at[pl.ds(0, 2)], self.second_last_sems.at[0])


def kernel(
    x_hbm, cot_hbm, sqkv_hbm, sout_hbm, tqkv_hbm, tout_hbm,
    grad_hbm, sgrad, tgrad,
    x, cot, qkv, sout, tout,
    packed, mixed, probs, temporal_probs, residual, residual_in, cot_in,
    res, cot_pos, packed_two, grad_mixed, mixed_two, grad_packed, grad_norm,
    back, back_in,
    t_part, t_first, t_wide, t_wide_last, t_second, t_second_last, t_final,
    s_part, s_first, s_wide, s_second, s_rest, s_block, s_third, s_last, s_final,
    load, swap, out_sem,
    cot_send, cot_recv, res_send, res_recv, back_send, back_recv,
    *sems,
):
    me, clip = lax.axis_index("seq"), lax.axis_index("dp")
    temporal_sum = RowsFirst(
        t_part, t_first, t_wide, t_wide_last, t_second, t_second_last, t_final, sems[:2], sems[4:10]
    )
    spatial_sum = TwoWays(
        s_part, s_first, s_wide, s_second, s_rest, s_block, s_third, s_last, s_final,
        sems[2:4], sems[10:],
    )
    factor = 1.0 / math.sqrt(TOKENS * SEQ * DP)

    qkv_chunks = chunks(3 * D, 768)

    def load_qkv(source, index):
        at, size = qkv_chunks[index]
        columns = pl.ds(at, size)
        return pltpu.make_async_copy(source.at[:, columns], qkv.at[:, columns], swap.at[index])

    load_x = pltpu.make_async_copy(x_hbm, x, load.at[0])
    load_cot = pltpu.make_async_copy(cot_hbm, cot, load.at[1])
    load_sout = pltpu.make_async_copy(sout_hbm, sout, load.at[2])
    load_tout = pltpu.make_async_copy(tout_hbm, tout, load.at[3])
    load_x.start()
    load_cot.start()
    for index in range(len(qkv_chunks)):
        load_qkv(sqkv_hbm, index).start()
    load_sout.start()

    barrier = pltpu.get_barrier_semaphore()

    def greet_seq(step, carry):
        pl.semaphore_signal(
            barrier, inc=1, device_id={"seq": lax.rem(me + step, SEQ)}, device_id_type=MESH
        )
        return carry

    def greet_dp(step, carry):
        pl.semaphore_signal(
            barrier, inc=1, device_id={"dp": lax.rem(clip + step, DP)}, device_id_type=MESH
        )
        return carry

    lax.fori_loop(1, SEQ, greet_seq, 0)
    lax.fori_loop(1, DP, greet_dp, 0)

    def send_cot(step, frame):
        peer = lax.rem(me + step, SEQ)
        return pltpu.make_async_remote_copy(
            src_ref=cot.at[frame, pl.ds(pl.multiple_of(16 * peer, 16), 16), :],
            dst_ref=cot_in.at[2 * me + frame],
            send_sem=cot_send.at[frame],
            recv_sem=cot_recv.at[frame],
            device_id={"seq": peer},
            device_id_type=MESH,
        )

    def send_residual(step, frame):
        peer = lax.rem(me + step, SEQ)
        return pltpu.make_async_remote_copy(
            src_ref=residual.at[frame, pl.ds(pl.multiple_of(16 * peer, 16), 16), :],
            dst_ref=residual_in.at[2 * me + frame],
            send_sem=res_send.at[frame],
            recv_sem=res_recv.at[frame],
            device_id={"seq": peer},
            device_id_type=MESH,
        )

    def send_back(step, group):
        peer = lax.rem(me + step, SEQ)
        return pltpu.make_async_remote_copy(
            src_ref=back.at[peer, group],
            dst_ref=back_in.at[me, group],
            send_sem=back_send.at[group],
            recv_sem=back_recv.at[group],
            device_id={"seq": peer},
            device_id_type=MESH,
        )

    def each(action):
        def body(step, carry):
            action(step)
            return carry

        lax.fori_loop(1, SEQ, body, 0)

    def exchanged(sem):
        settle(cot_in.at[pl.ds(0, SEQ - 1)], sem)

    load_x.wait()
    for frame in range(2):
        rows = slice(frame * HW, frame * HW + HW)
        norm, _ = rms_forward(x[frame])
        for index, (at, size) in enumerate(qkv_chunks):
            if frame == 0:
                load_qkv(sqkv_hbm, index).wait()
            if frame == 0 and index == 1:
                load_cot.wait()
                pl.semaphore_wait(barrier, SEQ - 1 + DP - 1)
                each(lambda step: send_cot(step, 0).start())
            packed[rows, at : at + size] = nn(norm, qkv[:, at : at + size]).astype(BF16)
        if frame == 0:
            cot_in[pl.ds(2 * me, 2)] = cot[:, pl.ds(pl.multiple_of(16 * me, 16), 16), :]
        else:
            for index in range(len(qkv_chunks)):
                load_qkv(tqkv_hbm, index).start()
            load_tout.start()
        spatial_forward(packed, mixed, probs, frame)
        if frame == 0:
            load_sout.wait()
        for at, size in chunks(D, 256):
            residual[frame, :, at : at + size] = (
                x[frame, :, at : at + size].astype(F32) + nn(mixed[rows, :], sout[:, at : at + size])
            ).astype(BF16)
        each(lambda step: send_residual(step, frame).start())
        residual_in[2 * me + frame] = residual[frame, pl.ds(pl.multiple_of(16 * me, 16), 16), :]

    each(lambda step: send_cot(step, 1).start())
    for frame in range(2):
        exchanged(res_recv.at[frame])

    orders = [
        one_hot(
            HW, TOKENS, lambda row, group=group: (row % FRAMES) * 16 + group * 8 + row // FRAMES
        )
        for group in range(2)
    ]
    inverses = []
    for group in range(2):
        rows = slice(group * HW, group * HW + HW)
        res[rows, :] = nn(orders[group], residual_in[...].reshape(TOKENS, D)).astype(BF16)
        norm, inverse = rms_forward(res[rows, :])
        inverses.append(inverse)
        for index, (at, size) in enumerate(qkv_chunks):
            if group == 0:
                load_qkv(tqkv_hbm, index).wait()
            packed_two[rows, at : at + size] = nn(norm, qkv[:, at : at + size]).astype(BF16)
        temporal_forward(packed_two, mixed_two, temporal_probs, group)

    load_tout.wait()
    for frame in range(2):
        exchanged(cot_recv.at[frame])
    for group in range(2):
        rows = slice(group * HW, group * HW + HW)
        cot_pos[rows, :] = nn(orders[group], cot_in[...].reshape(TOKENS, D)).astype(BF16)
        for at, size in chunks(D, 256):
            grad_mixed[rows, at : at + size] = nt(cot_pos[rows, :], tout[at : at + size, :]).astype(
                BF16
            )
        temporal_backward(packed_two, grad_mixed, grad_packed, temporal_probs, group)
        for at, size in chunks(D, 256):
            grad_norm[rows, at : at + size] = nt(grad_packed[...], qkv[at : at + size, :]).astype(
                BF16
            )
        if group == 1:
            for index in range(len(qkv_chunks)):
                load_qkv(sqkv_hbm, index).start()
        grad = (
            cot_pos[rows, :].astype(F32)
            + rms_backward(res[rows, :], grad_norm[rows, :], inverses[group])
        ).astype(BF16)
        order = one_hot(
            HW, HW, lambda row: (row % 8) * FRAMES + (row // 16) * 2 + (row // 8) % 2
        )
        back[:, group] = nn(order, grad).astype(BF16).reshape(SEQ, 16, D)
        each(lambda step: send_back(step, group).start())
        back_in[me, group] = back[me, group]

    temporal_sum.start(mixed_two, cot_pos)
    temporal_sum.over_cores()

    grad_res, grad_out = res, mixed_two
    for group in range(2):
        exchanged(back_recv.at[group])
    for frame in range(2):
        rows = slice(frame * HW, frame * HW + HW)
        order = one_hot(HW, TOKENS, lambda row, frame=frame: (row // 8) * 16 + frame * 8 + row % 8)
        grad_res[rows, :] = nn(order, back_in[...].reshape(TOKENS, D)).astype(BF16)
    spatial_sum.start(mixed, grad_res)

    def store(frame):
        return pltpu.make_async_copy(
            grad_out.at[pl.ds(frame * HW, HW)], grad_hbm.at[frame], out_sem.at[frame]
        )

    for at, size in chunks(D, 256):
        grad_mixed[:, at : at + size] = nt(grad_res[...], sout[at : at + size, :]).astype(BF16)
    spatial_sum.over_cores()
    for index in range(len(qkv_chunks)):
        load_qkv(sqkv_hbm, index).wait()
    for frame in range(2):
        rows = slice(frame * HW, frame * HW + HW)
        spatial_backward(packed, grad_mixed, grad_packed, probs, frame)
        for at, size in chunks(D, 256):
            grad_norm[rows, at : at + size] = nt(grad_packed[...], qkv[at : at + size, :]).astype(
                BF16
            )
        _, inverse = rms_forward(x[frame])
        grad_out[rows, :] = (
            grad_res[rows, :].astype(F32) + rms_backward(x[frame], grad_norm[rows, :], inverse)
        ).astype(BF16)
        store(frame).start()
        if frame == 0:
            temporal_sum.over_x()

    temporal_sum.over_seq()
    spatial_sum.second_stage()
    temporal_sum.finish(tgrad, factor)
    spatial_sum.third_stage()
    temporal_sum.drain()
    for frame in range(2):
        store(frame).wait()
        exchanged(cot_send.at[frame])
        exchanged(res_send.at[frame])
        exchanged(back_send.at[frame])
    spatial_sum.finish(sgrad, factor)
    spatial_sum.drain()


def local(layer_input, cotangent, spatial_qkv, spatial_out, temporal_qkv, temporal_out):
    def vmem(*shape, dtype=BF16):
        return pltpu.VMEM(shape, dtype)

    by_rows = [
        vmem(2, 2, 4, PADDED, D), vmem(2, 4, PADDED, D),
        vmem(4, 2, 4, PADDED, 256), vmem(4, 2, PADDED, 128),
        vmem(8, PADDED, 256), vmem(8, PADDED, 128), vmem(2, PADDED, D),
    ]
    two_ways = [
        vmem(2, 2, 4, PADDED, D), vmem(2, 4, PADDED, D),
        vmem(4, 2, 4, PADDED, 128), vmem(8, PADDED, 128), vmem(8, PADDED, 640),
        vmem(PADDED, 640), vmem(4, PADDED, 128), vmem(4, PADDED, 128), vmem(2, PADDED, D),
    ]
    dma = pltpu.SemaphoreType.DMA
    scratch = [
        vmem(2, HW, D), vmem(2, HW, D), vmem(D, 3 * D), vmem(D, D), vmem(D, D),
        vmem(TOKENS, 3 * D), vmem(TOKENS, D), vmem(2 * HEADS, HW, HW), vmem(2 * HEADS, FRAMES, HW),
        vmem(2, HW, D), vmem(FRAMES, 16, D), vmem(FRAMES, 16, D),
        vmem(TOKENS, D), vmem(TOKENS, D), vmem(TOKENS, 3 * D), vmem(TOKENS, D),
        vmem(TOKENS, D), vmem(HW, 3 * D), vmem(TOKENS, D),
        vmem(SEQ, 2, 16, D), vmem(SEQ, 2, 16, D),
        *by_rows,
        *two_ways,
        dma((4,)), dma((5,)), dma((2,)),
        *[dma((2,)) for _ in range(6)],
        *[dma(()), dma((8,))] * 2,
        *[dma((2,)) for _ in range(13)],
    ]
    hbm, on_chip = pl.BlockSpec(memory_space=pl.ANY), pl.BlockSpec(memory_space=pltpu.VMEM)
    grad, spatial_grad, temporal_grad = pl.pallas_call(
        kernel,
        out_shape=(
            jax.ShapeDtypeStruct((2, HW, D), BF16),
            jax.ShapeDtypeStruct((SHARE, D), F32),
            jax.ShapeDtypeStruct((SHARE, D), F32),
        ),
        in_specs=[hbm] * 6,
        out_specs=(hbm, on_chip, on_chip),
        scratch_shapes=scratch,
        compiler_params=pltpu.CompilerParams(
            collective_id=0, has_side_effects=True, vmem_limit_bytes=62 * 2**20
        ),
        cost_estimate=pl.CostEstimate(
            flops=40_000_000_000, bytes_accessed=40_000_000, transcendentals=3_000_000
        ),
        name="attention_pair_backward",
    )(
        layer_input.reshape(2, HW, D), cotangent.reshape(2, HW, D),
        spatial_qkv, spatial_out, temporal_qkv, temporal_out,
    )
    return grad.reshape(1, 2, HW, D), spatial_grad, temporal_grad


def solution(mesh):
    placed = (P("dp", "seq", None, None), P("dp", "seq", None, None), P(), P(), P(), P())
    return jax.shard_map(
        local,
        mesh=mesh,
        in_specs=placed,
        out_specs=(P("dp", "seq", None, None), P("seq", None), P("seq", None)),
        check_vma=False,
    )
```

```python
import functools
import math

import jax
import jax.numpy as jnp
from jax import lax
from jax.experimental import pallas as pl
from jax.experimental.pallas import tpu as pltpu
from jax.sharding import PartitionSpec as P

D = 1152
HEADS = 16
HEAD = D // HEADS
HW = 256
FRAMES = 32
SEQ = 16
DP = 8
TOKENS = 512
SHARE = D // SEQ
PADDED = 80
EPSILON = 1e-06
SCALE = 1.0 / math.sqrt(HEAD)
LOG2_E = math.log2(math.e)
F32 = jnp.float32
BF16 = jnp.bfloat16
MESH = pl.DeviceIdType.MESH
HALF = slice(0, HW)


def nn(left, right):
    return lax.dot_general(left, right, (((1,), (0,)), ((), ())), preferred_element_type=F32)


def nt(left, right):
    return lax.dot_general(left, right, (((1,), (1,)), ((), ())), preferred_element_type=F32)


def tn(left, right):
    return lax.dot_general(left, right, (((0,), (0,)), ((), ())), preferred_element_type=F32)


def chunks(width, step):
    return [(at, min(step, width - at)) for at in range(0, width, step)]


def rms_forward(block):
    widened = block.astype(F32)
    inverse = lax.rsqrt(jnp.mean(widened * widened, axis=-1, keepdims=True) + EPSILON)
    return (widened * inverse).astype(BF16), inverse


def rms_backward(block, grad_norm, inverse):
    widened = block.astype(F32)
    grad_wide = grad_norm.astype(F32)
    inner = jnp.mean(grad_wide * widened, axis=-1, keepdims=True)
    return inverse * grad_wide - widened * (inverse * inverse * inverse * inner)


def one_hot(rows, columns, target):
    row = lax.broadcasted_iota(jnp.int32, (rows, columns), 0)
    column = lax.broadcasted_iota(jnp.int32, (rows, columns), 1)
    return jnp.where(column == target(row), 1.0, 0.0).astype(BF16)


def pair_masks(pair):
    lane = lax.broadcasted_iota(jnp.int32, (1, 256), 1)
    first = (lane >= 16 * pair) & (lane < 16 * pair + HEAD)
    second = (lane >= 16 * pair + HEAD) & (lane < 16 * pair + 2 * HEAD)
    return first, second


def window(pair, base=0):
    return pl.ds(pl.multiple_of(128 * pair + base, 128), 256)


def tile(pair, base=0):
    return pl.ds(pl.multiple_of(128 * pair + base, 128), 128)


def pick(values, mask):
    return jnp.where(mask, values, jnp.zeros_like(values))


def put(ref, rows, base, pair, carry, result):
    ref[rows, tile(pair, base)] = (carry + result[:, :128]).astype(BF16)
    return result[:, 128:]


def softmax_keys(scores):
    top = jnp.max(scores, axis=0, keepdims=True)
    powers = jnp.exp2((scores - top) * (SCALE * LOG2_E))
    return powers * (1.0 / jnp.sum(powers, axis=0, keepdims=True))


def over_pairs(body, outputs):
    zero = jnp.zeros((HW, 128), F32)
    carries = lax.fori_loop(0, HEADS // 2, body, (zero,) * len(outputs), unroll=HEADS // 2)
    for (ref, rows, base), carry in zip(outputs, carries):
        ref[rows, base + 1024 : base + 1152] = carry.astype(BF16)


def half(ref, index, columns=slice(None)):
    return ref[8 * index : 8 * index + 8, :, :, columns].reshape(HW, -1)


def spatial_forward(packed, mixed, probs, frame):
    rows = slice(frame * HW, frame * HW + HW)

    def body(pair, carries):
        masks = pair_masks(pair)
        queries = packed[rows, window(pair)]
        keys = packed[rows, window(pair, D)]
        values = packed[rows, window(pair, 2 * D)]
        weights = []
        for index, mask in enumerate(masks):
            weight = softmax_keys(nt(pick(keys, mask), queries)).astype(BF16)
            probs[frame * HEADS + 2 * pair + index] = weight
            weights.append(weight)
        result = tn(
            jnp.concatenate(weights, axis=0),
            jnp.concatenate([pick(values, mask) for mask in masks], axis=0),
        )
        return (put(mixed, rows, 0, pair, carries[0], result),)

    over_pairs(body, [(mixed, rows, 0)])


def spatial_backward(packed, grad_mixed, grad_packed, probs, frame):
    rows = slice(frame * HW, frame * HW + HW)

    def body(pair, carries):
        masks = pair_masks(pair)
        queries = packed[rows, window(pair)]
        keys = packed[rows, window(pair, D)]
        values = packed[rows, window(pair, 2 * D)]
        grads = [pick(half(grad_mixed, frame, window(pair)), mask) for mask in masks]
        weights = [probs[frame * HEADS + 2 * pair + index] for index in range(2)]
        value_part = nn(jnp.concatenate(weights, axis=1), jnp.concatenate(grads, axis=0))
        scores = []
        for weight, grad in zip(weights, grads):
            grad_attention = nt(values, grad)
            wide = weight.astype(F32)
            inner = jnp.sum(wide * grad_attention, axis=0, keepdims=True)
            scores.append((wide * (grad_attention - inner) * SCALE).astype(BF16))
        query_part = tn(
            jnp.concatenate(scores, axis=0),
            jnp.concatenate([pick(keys, mask) for mask in masks], axis=0),
        )
        key_part = nn(
            jnp.concatenate(scores, axis=1),
            jnp.concatenate([pick(queries, mask) for mask in masks], axis=0),
        )
        return (
            put(grad_packed, HALF, 0, pair, carries[0], query_part),
            put(grad_packed, HALF, D, pair, carries[1], key_part),
            put(grad_packed, HALF, 2 * D, pair, carries[2], value_part),
        )

    over_pairs(body, [(grad_packed, HALF, base) for base in (0, D, 2 * D)])


def own_keys(scores, lane_block):
    kept = pick(scores[:FRAMES], lane_block == 0)
    for block in range(1, 8):
        kept = jnp.where(
            lane_block == block, scores[FRAMES * block : FRAMES * (block + 1)], kept
        )
    return kept


def all_keys(kept, lane_block):
    return jnp.concatenate([pick(kept, lane_block == block) for block in range(8)], axis=0)


def temporal_forward(packed, mixed, probs, group):
    rows = slice(group * HW, group * HW + HW)

    def body(pair, carries):
        masks = pair_masks(pair)
        lane_block = lax.broadcasted_iota(jnp.int32, (1, 256), 1) // FRAMES
        queries = half(packed, group, window(pair))
        keys = half(packed, group, window(pair, D))
        values = half(packed, group, window(pair, 2 * D))
        weights = []
        for index, mask in enumerate(masks):
            weight = softmax_keys(own_keys(nt(pick(keys, mask), queries), lane_block)).astype(BF16)
            probs[group * HEADS + 2 * pair + index] = weight
            weights.append(all_keys(weight, lane_block))
        result = tn(
            jnp.concatenate(weights, axis=0),
            jnp.concatenate([pick(values, mask) for mask in masks], axis=0),
        )
        return (put(mixed, rows, 0, pair, carries[0], result),)

    over_pairs(body, [(mixed, rows, 0)])


def temporal_backward(packed, grad_mixed, grad_packed, probs, group):
    def body(pair, carries):
        masks = pair_masks(pair)
        lane_block = lax.broadcasted_iota(jnp.int32, (1, 256), 1) // FRAMES
        queries = half(packed, group, window(pair))
        keys = half(packed, group, window(pair, D))
        values = half(packed, group, window(pair, 2 * D))
        grads = [pick(half(grad_mixed, group, window(pair)), mask) for mask in masks]
        weights, scores = [], []
        for index, grad in enumerate(grads):
            weight = probs[group * HEADS + 2 * pair + index]
            grad_attention = own_keys(nt(values, grad), lane_block)
            wide = weight.astype(F32)
            inner = jnp.sum(wide * grad_attention, axis=0, keepdims=True)
            score = (wide * (grad_attention - inner) * SCALE).astype(BF16)
            weights.append(all_keys(weight, lane_block))
            scores.append(all_keys(score, lane_block))
        value_part = nn(jnp.concatenate(weights, axis=1), jnp.concatenate(grads, axis=0))
        query_part = tn(
            jnp.concatenate(scores, axis=0),
            jnp.concatenate([pick(keys, mask) for mask in masks], axis=0),
        )
        key_part = nn(
            jnp.concatenate(scores, axis=1),
            jnp.concatenate([pick(queries, mask) for mask in masks], axis=0),
        )
        return (
            put(grad_packed, HALF, 0, pair, carries[0], query_part),
            put(grad_packed, HALF, D, pair, carries[1], key_part),
            put(grad_packed, HALF, 2 * D, pair, carries[2], value_part),
        )

    over_pairs(body, [(grad_packed, HALF, base) for base in (0, D, 2 * D)])


def weight_shares(left, right, part, ready):
    tail, at = None, 0
    for chunk in range(3):
        product = tn(left[:, 384 * chunk : 384 * chunk + 384], right[...])
        if tail is not None:
            product = jnp.concatenate([tail, product], axis=0)
        count = product.shape[0] // SHARE
        for index in range(count):
            share = product[SHARE * index : SHARE * index + SHARE]
            padding = jnp.zeros((PADDED - SHARE, D), F32)
            core, chip = (at + index) % 2, (at + index) // 2
            part[core, chip // 4, chip % 4] = jnp.concatenate([share, padding], axis=0).astype(BF16)
        for chip in range(at // 2, (at + count) // 2):
            ready(chip)
        at += count
        tail = product[SHARE * count :] if at < SEQ else None


def settle(ref, sem):
    pltpu.make_async_copy(ref, ref, sem).wait()


class Reduction:
    def __init__(self, part, first, sems):
        self.part, self.first = part, first
        self.first_send, self.first_recv = sems
        self.me = lax.axis_index("seq")
        self.clip = lax.axis_index("dp")
        self.core = lax.rem(self.me, 2)
        self.chip = self.me // 2
        self.along_x = lax.rem(self.clip, 4)
        self.along_y = self.clip // 4
        self.along_z = lax.rem(self.chip, 4)

    def copy(self, source, target, send, recv, device):
        return pltpu.make_async_remote_copy(
            src_ref=source,
            dst_ref=target,
            send_sem=send,
            recv_sem=recv,
            device_id=device,
            device_id_type=MESH,
        )

    def x_peer(self, step):
        return lax.rem(self.along_x + step, 4)

    def to_x(self, step, source, target, sems):
        device = {"dp": 4 * self.along_y + self.x_peer(step)}
        self.copy(source, target, sems.at[0], sems.at[1], device).start()

    def to_seq(self, step, source, target, sems):
        device = {"seq": 2 * lax.rem(self.chip + step, 8) + self.core}
        self.copy(source, target, sems.at[0], sems.at[1], device).start()

    def to_dp(self, step, place, sems):
        device = {"dp": lax.rem(self.clip + step, DP)}
        self.copy(place, place, sems.at[0], sems.at[1], device).start()

    def to_core(self, chip):
        return self.copy(
            self.part.at[1 - self.core, chip // 4, lax.rem(chip, 4)],
            self.first.at[chip // 4, lax.rem(chip, 4)],
            self.first_send,
            self.first_recv.at[chip],
            {"seq": self.me + 1 - 2 * self.core},
        )

    def start(self, left, right):
        weight_shares(left, right, self.part, lambda chip: self.to_core(chip).start())

    def add_cores(self, chip):
        self.to_core(chip).wait_recv()
        high, low = chip // 4, lax.rem(chip, 4)
        total = self.part[self.core, high, low].astype(F32) + self.first[high, low].astype(F32)
        self.part[self.core, high, low] = total.astype(BF16)

    def lanes(self, at, width):
        return pl.ds(pl.multiple_of(at, 128), width)

    def finish(self, out, factor):
        self.settle_all()
        total = self.final[0, :SHARE, :].astype(F32) + self.final[1, :SHARE, :].astype(F32)
        out[...] = total * factor


class TwoWays(Reduction):
    def __init__(self, part, first, wide, second, rest, block, third, last, final, sems, pairs):
        super().__init__(part, first, sems)
        self.wide, self.second, self.rest = wide, second, rest
        self.block, self.third, self.last, self.final = block, third, last, final
        (self.wide_sems, self.second_sems, self.rest_sems, self.third_sems, self.last_sems,
         self.final_sems, self.end_sems) = pairs

    def over_cores(self):
        def send(step, carry):
            chip = lax.rem(self.chip + step, 8)
            self.add_cores(chip)

            @pl.when(step < 8)
            def _():
                source = self.part.at[self.core, chip // 4, lax.rem(chip, 4), :, pl.ds(512, 640)]
                self.to_seq(step, source, self.rest.at[step], self.rest_sems)

            return carry

        lax.fori_loop(1, 9, send, 0)
        for step in range(1, 4):
            columns = self.lanes(128 * self.x_peer(step), 128)
            source = self.part.at[self.core, :, :, :, columns]
            self.to_x(step, source, self.wide.at[self.along_x], self.wide_sems)

    def second_stage(self):
        settle(self.wide.at[pl.ds(0, 3)], self.wide_sems.at[1])
        columns = self.lanes(128 * self.along_x, 128)
        total = self.part[self.core, :, :, :, columns].astype(F32)
        for step in range(1, 4):
            total = total + self.wide[self.x_peer(step)].astype(F32)
        self.wide[self.along_x] = total.astype(BF16)

        def send(step, carry):
            chip = lax.rem(self.chip + step, 8)
            source = self.wide.at[self.along_x, chip // 4, lax.rem(chip, 4)]
            self.to_seq(step, source, self.second.at[step], self.second_sems)
            return carry

        lax.fori_loop(1, 8, send, 0)
        settle(self.rest.at[pl.ds(1, 7)], self.rest_sems.at[1])
        total = self.part[self.core, self.chip // 4, self.along_z, :, 512:1152].astype(F32)
        for step in range(1, 8):
            total = total + self.rest[step].astype(F32)
        self.block[...] = total.astype(BF16)
        self.third[self.along_x] = self.block[:, columns]
        self.last[self.along_x] = self.block[:, 512:640]
        for step in range(1, 4):
            source = self.block.at[:, self.lanes(128 * self.x_peer(step), 128)]
            self.to_x(step, source, self.third.at[self.along_x], self.third_sems)
            source = self.block.at[:, pl.ds(512, 128)]
            self.to_x(step, source, self.last.at[self.along_x], self.last_sems)

    def third_stage(self):
        first, other = self.lanes(128 * self.along_x, 128), self.lanes(512 + 128 * self.along_x, 128)
        settle(self.second.at[pl.ds(1, 7)], self.second_sems.at[1])
        total = self.wide[self.along_x, self.chip // 4, self.along_z].astype(F32)
        for step in range(1, 8):
            total = total + self.second[step].astype(F32)
        self.final[self.along_y, :, first] = total.astype(BF16)
        for step in range(1, DP):
            self.to_dp(step, self.final.at[self.along_y, :, first], self.final_sems)
        settle(self.third.at[pl.ds(0, 3)], self.third_sems.at[1])
        settle(self.last.at[pl.ds(0, 3)], self.last_sems.at[1])
        total, last = self.third[0].astype(F32), self.last[0].astype(F32)
        for source in range(1, 4):
            total = total + self.third[source].astype(F32)
            last = last + self.last[source].astype(F32)
        self.final[self.along_y, :, other] = total.astype(BF16)
        self.final[self.along_y, :, 1024:1152] = last.astype(BF16)
        for step in range(1, DP):
            self.to_dp(step, self.final.at[self.along_y, :, other], self.final_sems)
        self.to_dp(4, self.final.at[self.along_y, :, pl.ds(1024, 128)], self.end_sems)

    def settle_all(self):
        settle(self.rest.at[pl.ds(0, 7), :, pl.ds(0, 256)], self.final_sems.at[1])
        settle(self.second.at[0], self.end_sems.at[1])

    def drain(self):
        settle(self.first, self.first_send)
        settle(self.rest.at[pl.ds(1, 7)], self.rest_sems.at[0])
        settle(self.wide.at[pl.ds(0, 3)], self.wide_sems.at[0])
        settle(self.second.at[pl.ds(1, 7)], self.second_sems.at[0])
        settle(self.third.at[pl.ds(0, 3)], self.third_sems.at[0])
        settle(self.last.at[pl.ds(0, 3)], self.last_sems.at[0])
        settle(self.rest.at[pl.ds(0, 7), :, pl.ds(0, 256)], self.final_sems.at[0])
        settle(self.second.at[0], self.end_sems.at[0])


class RowsFirst(Reduction):
    def __init__(self, part, first, wide, wide_last, second, second_last, final, sems, pairs):
        super().__init__(part, first, sems)
        self.wide, self.wide_last = wide, wide_last
        self.second, self.second_last, self.final = second, second_last, final
        (self.wide_sems, self.wide_last_sems, self.second_sems, self.second_last_sems,
         self.final_sems, self.final_last_sems) = pairs

    def over_cores(self):
        def add(chip, carry):
            self.add_cores(chip)
            return carry

        lax.fori_loop(0, 8, add, 0)
        for step in range(1, 4):
            peer = self.x_peer(step)
            source = self.part.at[self.core, :, :, :, self.lanes(256 * peer, 256)]
            self.to_x(step, source, self.wide.at[self.along_x], self.wide_sems)
            source = self.part.at[self.core, :, peer, :, pl.ds(1024, 128)]
            self.to_x(step, source, self.wide_last.at[self.along_x], self.wide_last_sems)

    def with_last(self, step):
        return lax.rem(self.chip + step, 4) == self.along_x

    def over_x(self):
        settle(self.wide.at[pl.ds(0, 3)], self.wide_sems.at[1])
        settle(self.wide_last.at[pl.ds(0, 3)], self.wide_last_sems.at[1])
        for high in range(2):
            columns = self.lanes(256 * self.along_x, 256)
            total = self.part[self.core, high, :, :, columns].astype(F32)
            last = self.part[self.core, high, self.along_x, :, 1024:1152].astype(F32)
            for step in range(1, 4):
                total = total + self.wide[self.x_peer(step), high].astype(F32)
                last = last + self.wide_last[self.x_peer(step), high].astype(F32)
            self.wide[self.along_x, high] = total.astype(BF16)
            self.wide_last[self.along_x, high] = last.astype(BF16)

        def send(step, carry):
            chip = lax.rem(self.chip + step, 8)
            source = self.wide.at[self.along_x, chip // 4, lax.rem(chip, 4)]
            self.to_seq(step, source, self.second.at[step], self.second_sems)

            @pl.when(self.with_last(step))
            def _():
                source = self.wide_last.at[self.along_x, chip // 4]
                self.to_seq(step, source, self.second_last.at[step], self.second_last_sems)

            return carry

        lax.fori_loop(1, 8, send, 0)

    def over_seq(self):
        high = self.chip // 4
        columns = self.lanes(256 * self.along_x, 256)
        settle(self.second.at[pl.ds(1, 7)], self.second_sems.at[1])
        total = self.wide[self.along_x, high, self.along_z].astype(F32)
        for step in range(1, 8):
            total = total + self.second[step].astype(F32)
        self.final[self.along_y, :, columns] = total.astype(BF16)
        for step in range(1, DP):
            self.to_dp(step, self.final.at[self.along_y, :, columns], self.final_sems)

        @pl.when(self.along_z == self.along_x)
        def _():
            settle(self.second_last.at[pl.ds(1, 7)], self.second_last_sems.at[1])
            last = self.wide_last[self.along_x, high].astype(F32)
            for step in range(1, 8):
                last = last + self.second_last[step].astype(F32)
            self.final[self.along_y, :, 1024:1152] = last.astype(BF16)
            for step in range(1, DP):
                place = self.final.at[self.along_y, :, pl.ds(1024, 128)]
                self.to_dp(step, place, self.final_last_sems)

    def settle_all(self):
        settle(self.second.at[pl.ds(0, 7)], self.final_sems.at[1])

        @pl.when(self.along_z == self.along_x)
        def _():
            settle(self.second_last.at[0], self.final_last_sems.at[1])

        @pl.when(self.along_z != self.along_x)
        def _():
            settle(self.second_last.at[pl.ds(0, 2)], self.final_last_sems.at[1])

    def drain(self):
        settle(self.first, self.first_send)
        settle(self.wide.at[pl.ds(0, 3)], self.wide_sems.at[0])
        settle(self.wide_last.at[pl.ds(0, 3)], self.wide_last_sems.at[0])
        settle(self.second.at[pl.ds(1, 7)], self.second_sems.at[0])
        settle(self.second.at[pl.ds(0, 7)], self.final_sems.at[0])

        @pl.when(self.along_z == self.along_x)
        def _():
            settle(self.second_last.at[0], self.second_last_sems.at[0])
            settle(self.second_last.at[pl.ds(0, 7)], self.final_last_sems.at[0])

        @pl.when(self.along_z != self.along_x)
        def _():
            settle(self.second_last.at[pl.ds(0, 2)], self.second_last_sems.at[0])


def kernel(
    x_hbm, cot_hbm, sqkv_hbm, sout_hbm, tqkv_hbm, tout_hbm,
    grad_hbm, sgrad, tgrad,
    x, cot, qkv, sout, tout,
    packed, mixed, probs, temporal_probs, residual, residual_in, cot_in, mixed_in,
    res, cot_pos, packed_two, grad_mixed, mixed_two, grad_packed, grad_norm,
    back, back_in,
    t_part, t_first, t_wide, t_wide_last, t_second, t_second_last, t_final,
    s_part, s_first, s_wide, s_second, s_rest, s_block, s_third, s_last, s_final,
    load, swap, out_sem,
    cot_send, cot_recv, res_send, res_recv, back_send, back_recv, mixed_send, mixed_recv,
    *sems,
):
    me, clip = lax.axis_index("seq"), lax.axis_index("dp")
    temporal_sum = RowsFirst(
        t_part, t_first, t_wide, t_wide_last, t_second, t_second_last, t_final, sems[:2], sems[4:10]
    )
    spatial_sum = TwoWays(
        s_part, s_first, s_wide, s_second, s_rest, s_block, s_third, s_last, s_final,
        sems[2:4], sems[10:],
    )
    factor = 1.0 / math.sqrt(TOKENS * SEQ * DP)

    qkv_chunks = chunks(3 * D, 768)

    def load_qkv(source, index):
        at, size = qkv_chunks[index]
        columns = pl.ds(at, size)
        return pltpu.make_async_copy(source.at[:, columns], qkv.at[:, columns], swap.at[index])

    load_x = pltpu.make_async_copy(x_hbm, x, load.at[0])
    load_cot = pltpu.make_async_copy(cot_hbm, cot, load.at[1])
    load_sout = pltpu.make_async_copy(sout_hbm, sout, load.at[2])
    load_tout = pltpu.make_async_copy(tout_hbm, tout, load.at[3])
    load_x.start()
    load_cot.start()
    for index in range(len(qkv_chunks)):
        load_qkv(sqkv_hbm, index).start()
    load_sout.start()

    barrier = pltpu.get_barrier_semaphore()

    def greet_seq(step, carry):
        pl.semaphore_signal(
            barrier, inc=1, device_id={"seq": lax.rem(me + step, SEQ)}, device_id_type=MESH
        )
        return carry

    def greet_dp(step, carry):
        pl.semaphore_signal(
            barrier, inc=1, device_id={"dp": lax.rem(clip + step, DP)}, device_id_type=MESH
        )
        return carry

    lax.fori_loop(1, SEQ, greet_seq, 0)
    lax.fori_loop(1, DP, greet_dp, 0)

    def send_cot(peer, frame):
        return pltpu.make_async_remote_copy(
            src_ref=cot.at[frame, pl.ds(pl.multiple_of(16 * peer, 16), 16), :],
            dst_ref=cot_in.at[frame, me],
            send_sem=cot_send.at[frame],
            recv_sem=cot_recv.at[frame],
            device_id={"seq": peer},
            device_id_type=MESH,
        )

    def send_residual(peer, frame):
        return pltpu.make_async_remote_copy(
            src_ref=residual.at[frame, pl.ds(pl.multiple_of(16 * peer, 16), 16), :],
            dst_ref=residual_in.at[frame, me],
            send_sem=res_send.at[frame],
            recv_sem=res_recv.at[frame],
            device_id={"seq": peer},
            device_id_type=MESH,
        )

    def send_back(peer, group):
        return pltpu.make_async_remote_copy(
            src_ref=back.at[peer, group],
            dst_ref=back_in.at[me, group],
            send_sem=back_send.at[group],
            recv_sem=back_recv.at[group],
            device_id={"seq": peer},
            device_id_type=MESH,
        )

    def send_mixed(peer, frame):
        return pltpu.make_async_remote_copy(
            src_ref=mixed.at[pl.ds(pl.multiple_of(frame * HW + 16 * peer, 16), 16)],
            dst_ref=mixed_in.at[frame, me],
            send_sem=mixed_send.at[frame],
            recv_sem=mixed_recv.at[frame],
            device_id={"seq": peer},
            device_id_type=MESH,
        )

    def each(action):
        high, low, core = me // 8, lax.rem(me, 8) // 2, lax.rem(me, 2)
        for turn, count in ((2, 4), (1, 4), (3, 4), (0, 3)):

            def body(index, carry, turn=turn):
                chip = 4 * lax.rem(high + 1 - index // 2, 2) + lax.rem(low + turn, 4)
                action(2 * chip + lax.rem(core + 1 - lax.rem(index, 2), 2))
                return carry

            lax.fori_loop(0, count, body, 0)

    def exchanged(sem):
        settle(cot_in.at[0, pl.ds(0, SEQ - 1)], sem)

    load_x.wait()
    for frame in range(2):
        rows = slice(frame * HW, frame * HW + HW)
        norm, _ = rms_forward(x[frame])
        for index, (at, size) in enumerate(qkv_chunks):
            if frame == 0:
                load_qkv(sqkv_hbm, index).wait()
            if frame == 0 and index == 1:
                load_cot.wait()
                pl.semaphore_wait(barrier, SEQ - 1 + DP - 1)
                each(lambda peer: send_cot(peer, 0).start())
            packed[rows, at : at + size] = nn(norm, qkv[:, at : at + size]).astype(BF16)
        if frame == 0:
            cot_in[:, me] = cot[:, pl.ds(pl.multiple_of(16 * me, 16), 16), :]
        else:
            for index in range(len(qkv_chunks)):
                load_qkv(tqkv_hbm, index).start()
            load_tout.start()
        spatial_forward(packed, mixed, probs, frame)
        if frame == 0:
            load_sout.wait()
        for at, size in chunks(D, 256):
            residual[frame, :, at : at + size] = (
                x[frame, :, at : at + size].astype(F32) + nn(mixed[rows, :], sout[:, at : at + size])
            ).astype(BF16)
        each(lambda peer: send_residual(peer, frame).start())
        residual_in[frame, me] = residual[frame, pl.ds(pl.multiple_of(16 * me, 16), 16), :]

    each(lambda peer: send_cot(peer, 1).start())
    for frame in range(2):
        each(lambda peer: send_mixed(peer, frame).start())
        mixed_in[frame, me] = mixed[pl.ds(pl.multiple_of(frame * HW + 16 * me, 16), 16), :]

    by_position = one_hot(HW, HW, lambda row: (row % SEQ) * 16 + row // SEQ)

    def positions(source, parity):
        return nn(by_position, source[parity].reshape(HW, D)).astype(BF16)

    def spread(values):
        return values.astype(BF16).reshape(16, SEQ, -1)

    def grads_of_mixed(parity):
        exchanged(cot_recv.at[parity])
        rows = positions(cot_in, parity)
        cot_pos[:, parity] = spread(rows)
        for at, size in chunks(D, 256):
            grad_mixed[:, parity, :, at : at + size] = spread(nt(rows, tout[at : at + size, :]))

    for parity in range(2):
        exchanged(res_recv.at[parity])
        rows = positions(residual_in, parity)
        res[:, parity] = spread(rows)
        norm, _ = rms_forward(rows)
        for index, (at, size) in enumerate(qkv_chunks):
            if parity == 0:
                load_qkv(tqkv_hbm, index).wait()
            packed_two[:, parity, :, at : at + size] = spread(nn(norm, qkv[:, at : at + size]))
        if parity == 0:
            load_tout.wait()
            grads_of_mixed(0)
    for group in range(2):
        temporal_forward(packed_two, mixed_two, temporal_probs, group)

    grads_of_mixed(1)
    for group in range(2):
        temporal_backward(packed_two, grad_mixed, grad_packed, temporal_probs, group)
        if group == 1:
            temporal_sum.over_cores()
        for at, size in chunks(D, 256):
            grad_norm[:, at : at + size] = nt(grad_packed[...], qkv[at : at + size, :]).astype(BF16)
        if group == 1:
            for index in range(len(qkv_chunks)):
                load_qkv(sqkv_hbm, index).start()
        rows = half(res, group)
        _, inverse = rms_forward(rows)
        grad = (
            half(cot_pos, group).astype(F32) + rms_backward(rows, grad_norm[...], inverse)
        ).astype(BF16)
        order = one_hot(
            HW, HW, lambda row: (row % 8) * FRAMES + ((row // 8) % 2) * 16 + row // 16
        )
        back[:, group] = nn(order, grad).astype(BF16).reshape(SEQ, 16, D)
        each(lambda peer: send_back(peer, group).start())
        back_in[me, group] = back[me, group]
        grad_mixed[8 * group : 8 * group + 8] = grad.reshape(8, 2, SEQ, D)
        if group == 0:
            temporal_sum.start(mixed_two, cot_pos[...].reshape(TOKENS, D))

    for frame in range(2):
        exchanged(mixed_recv.at[frame])
    for group in range(2):
        rows = slice(group * HW, group * HW + HW)
        order = one_hot(
            HW,
            TOKENS,
            lambda row, group=group: (
                (row // 16) % 2 * HW + (row % 16) * 16 + group * 8 + row // FRAMES
            ),
        )
        mixed_two[rows, :] = nn(order, mixed_in[...].reshape(TOKENS, D)).astype(BF16)
    spatial_sum.start(mixed_two, grad_mixed[...].reshape(TOKENS, D))
    spatial_sum.over_cores()

    grad_res, grad_out = res, mixed_two
    for group in range(2):
        exchanged(back_recv.at[group])
    for frame in range(2):
        rows = slice(frame * HW, frame * HW + HW)
        order = one_hot(HW, TOKENS, lambda row, frame=frame: (row // 8) * 16 + frame * 8 + row % 8)
        grad_res[8 * frame : 8 * frame + 8] = (
            nn(order, back_in[...].reshape(TOKENS, D)).astype(BF16).reshape(8, 2, SEQ, D)
        )

    def store(frame):
        return pltpu.make_async_copy(
            grad_out.at[pl.ds(frame * HW, HW)], grad_hbm.at[frame], out_sem.at[frame]
        )

    for at, size in chunks(D, 256):
        product = nt(grad_res[...].reshape(TOKENS, D), sout[at : at + size, :])
        grad_mixed[:, :, :, at : at + size] = product.astype(BF16).reshape(16, 2, SEQ, size)
    temporal_sum.over_x()
    for index in range(len(qkv_chunks)):
        load_qkv(sqkv_hbm, index).wait()
    for frame in range(2):
        rows = slice(frame * HW, frame * HW + HW)
        spatial_backward(packed, grad_mixed, grad_packed, probs, frame)
        for at, size in chunks(D, 256):
            grad_norm[:, at : at + size] = nt(grad_packed[...], qkv[at : at + size, :]).astype(BF16)
        _, inverse = rms_forward(x[frame])
        grad_out[rows, :] = (
            half(grad_res, frame).astype(F32) + rms_backward(x[frame], grad_norm[...], inverse)
        ).astype(BF16)
        store(frame).start()
        if frame == 0:
            temporal_sum.over_seq()

    spatial_sum.second_stage()
    spatial_sum.third_stage()
    temporal_sum.finish(tgrad, factor)
    temporal_sum.drain()
    for frame in range(2):
        store(frame).wait()
        exchanged(cot_send.at[frame])
        exchanged(res_send.at[frame])
        exchanged(back_send.at[frame])
        exchanged(mixed_send.at[frame])
    spatial_sum.finish(sgrad, factor)
    spatial_sum.drain()


def local(layer_input, cotangent, spatial_qkv, spatial_out, temporal_qkv, temporal_out):
    def vmem(*shape, dtype=BF16):
        return pltpu.VMEM(shape, dtype)

    by_rows = [
        vmem(2, 2, 4, PADDED, D), vmem(2, 4, PADDED, D),
        vmem(4, 2, 4, PADDED, 256), vmem(4, 2, PADDED, 128),
        vmem(8, PADDED, 256), vmem(8, PADDED, 128), vmem(2, PADDED, D),
    ]
    two_ways = [
        vmem(2, 2, 4, PADDED, D), vmem(2, 4, PADDED, D),
        vmem(4, 2, 4, PADDED, 128), vmem(8, PADDED, 128), vmem(8, PADDED, 640),
        vmem(PADDED, 640), vmem(4, PADDED, 128), vmem(4, PADDED, 128), vmem(2, PADDED, D),
    ]
    dma = pltpu.SemaphoreType.DMA
    scratch = [
        vmem(2, HW, D), vmem(2, HW, D), vmem(D, 3 * D), vmem(D, D), vmem(D, D),
        vmem(TOKENS, 3 * D), vmem(TOKENS, D), vmem(2 * HEADS, HW, HW), vmem(2 * HEADS, FRAMES, HW),
        vmem(2, HW, D), *[vmem(2, SEQ, 16, D) for _ in range(3)],
        vmem(16, 2, SEQ, D), vmem(16, 2, SEQ, D), vmem(16, 2, SEQ, 3 * D), vmem(16, 2, SEQ, D),
        vmem(TOKENS, D), vmem(HW, 3 * D), vmem(HW, D),
        vmem(SEQ, 2, 16, D), vmem(SEQ, 2, 16, D),
        *by_rows,
        *two_ways,
        dma((4,)), dma((5,)), dma((2,)),
        *[dma((2,)) for _ in range(8)],
        *[dma(()), dma((8,))] * 2,
        *[dma((2,)) for _ in range(13)],
    ]
    hbm, on_chip = pl.BlockSpec(memory_space=pl.ANY), pl.BlockSpec(memory_space=pltpu.VMEM)
    grad, spatial_grad, temporal_grad = pl.pallas_call(
        kernel,
        out_shape=(
            jax.ShapeDtypeStruct((2, HW, D), BF16),
            jax.ShapeDtypeStruct((SHARE, D), F32),
            jax.ShapeDtypeStruct((SHARE, D), F32),
        ),
        in_specs=[hbm] * 6,
        out_specs=(hbm, on_chip, on_chip),
        scratch_shapes=scratch,
        compiler_params=pltpu.CompilerParams(
            collective_id=0, has_side_effects=True, vmem_limit_bytes=62 * 2**20
        ),
        cost_estimate=pl.CostEstimate(
            flops=40_000_000_000, bytes_accessed=40_000_000, transcendentals=3_000_000
        ),
        name="attention_pair_backward",
    )(
        layer_input.reshape(2, HW, D), cotangent.reshape(2, HW, D),
        spatial_qkv, spatial_out, temporal_qkv, temporal_out,
    )
    return grad.reshape(1, 2, HW, D), spatial_grad, temporal_grad


def solution(mesh):
    placed = (P("dp", "seq", None, None), P("dp", "seq", None, None), P(), P(), P(), P())
    return jax.shard_map(
        local,
        mesh=mesh,
        in_specs=placed,
        out_specs=(P("dp", "seq", None, None), P("seq", None), P("seq", None)),
        check_vma=False,
    )
```

```python
import functools
import math

import jax
import jax.numpy as jnp
from jax import lax
from jax.experimental import pallas as pl
from jax.experimental.pallas import tpu as pltpu
from jax.sharding import PartitionSpec as P

D = 1152
HEADS = 16
HEAD = D // HEADS
HW = 256
FRAMES = 32
SEQ = 16
DP = 8
TOKENS = 512
SHARE = D // SEQ
PADDED = 80
EPSILON = 1e-06
SCALE = 1.0 / math.sqrt(HEAD)
LOG2_E = math.log2(math.e)
F32 = jnp.float32
BF16 = jnp.bfloat16
MESH = pl.DeviceIdType.MESH
HALF = slice(0, HW)


def nn(left, right):
    return lax.dot_general(left, right, (((1,), (0,)), ((), ())), preferred_element_type=F32)


def nt(left, right):
    return lax.dot_general(left, right, (((1,), (1,)), ((), ())), preferred_element_type=F32)


def tn(left, right):
    return lax.dot_general(left, right, (((0,), (0,)), ((), ())), preferred_element_type=F32)


def chunks(width, step):
    return [(at, min(step, width - at)) for at in range(0, width, step)]


def rms_forward(block):
    widened = block.astype(F32)
    inverse = lax.rsqrt(jnp.mean(widened * widened, axis=-1, keepdims=True) + EPSILON)
    return (widened * inverse).astype(BF16), inverse


def rms_backward(block, grad_norm, inverse):
    widened = block.astype(F32)
    grad_wide = grad_norm.astype(F32)
    inner = jnp.mean(grad_wide * widened, axis=-1, keepdims=True)
    return inverse * grad_wide - widened * (inverse * inverse * inverse * inner)


def one_hot(rows, columns, target):
    row = lax.broadcasted_iota(jnp.int32, (rows, columns), 0)
    column = lax.broadcasted_iota(jnp.int32, (rows, columns), 1)
    return jnp.where(column == target(row), 1.0, 0.0).astype(BF16)


def pair_masks(pair):
    lane = lax.broadcasted_iota(jnp.int32, (1, 256), 1)
    first = (lane >= 16 * pair) & (lane < 16 * pair + HEAD)
    second = (lane >= 16 * pair + HEAD) & (lane < 16 * pair + 2 * HEAD)
    return first, second


def window(pair, base=0):
    return pl.ds(pl.multiple_of(128 * pair + base, 128), 256)


def tile(pair, base=0):
    return pl.ds(pl.multiple_of(128 * pair + base, 128), 128)


def pick(values, mask):
    return jnp.where(mask, values, jnp.zeros_like(values))


def put(ref, rows, base, pair, carry, result):
    ref[rows, tile(pair, base)] = (carry + result[:, :128]).astype(BF16)
    return result[:, 128:]


def softmax_keys(scores):
    top = jnp.max(scores, axis=0, keepdims=True)
    powers = jnp.exp2((scores - top) * (SCALE * LOG2_E))
    return powers * (1.0 / jnp.sum(powers, axis=0, keepdims=True))


def over_pairs(body, outputs):
    zero = jnp.zeros((HW, 128), F32)
    carries = lax.fori_loop(0, HEADS // 2, body, (zero,) * len(outputs), unroll=HEADS // 2)
    for (ref, rows, base), carry in zip(outputs, carries):
        ref[rows, base + 1024 : base + 1152] = carry.astype(BF16)


def half(ref, index, columns=slice(None)):
    return ref[8 * index : 8 * index + 8, :, :, columns].reshape(HW, -1)


def spatial_forward(packed, mixed, probs, frame):
    rows = slice(frame * HW, frame * HW + HW)

    def body(pair, carries):
        masks = pair_masks(pair)
        queries = packed[rows, window(pair)]
        keys = packed[rows, window(pair, D)]
        values = packed[rows, window(pair, 2 * D)]
        weights = []
        for index, mask in enumerate(masks):
            weight = softmax_keys(nt(pick(keys, mask), queries)).astype(BF16)
            probs[frame * HEADS + 2 * pair + index] = weight
            weights.append(weight)
        result = tn(
            jnp.concatenate(weights, axis=0),
            jnp.concatenate([pick(values, mask) for mask in masks], axis=0),
        )
        return (put(mixed, rows, 0, pair, carries[0], result),)

    over_pairs(body, [(mixed, rows, 0)])


def spatial_backward(packed, grad_mixed, grad_packed, probs, frame):
    rows = slice(frame * HW, frame * HW + HW)

    def body(pair, carries):
        masks = pair_masks(pair)
        queries = packed[rows, window(pair)]
        keys = packed[rows, window(pair, D)]
        values = packed[rows, window(pair, 2 * D)]
        grads = [pick(half(grad_mixed, frame, window(pair)), mask) for mask in masks]
        weights = [probs[frame * HEADS + 2 * pair + index] for index in range(2)]
        value_part = nn(jnp.concatenate(weights, axis=1), jnp.concatenate(grads, axis=0))
        scores = []
        for weight, grad in zip(weights, grads):
            grad_attention = nt(values, grad)
            wide = weight.astype(F32)
            inner = jnp.sum(wide * grad_attention, axis=0, keepdims=True)
            scores.append((wide * (grad_attention - inner) * SCALE).astype(BF16))
        query_part = tn(
            jnp.concatenate(scores, axis=0),
            jnp.concatenate([pick(keys, mask) for mask in masks], axis=0),
        )
        key_part = nn(
            jnp.concatenate(scores, axis=1),
            jnp.concatenate([pick(queries, mask) for mask in masks], axis=0),
        )
        return (
            put(grad_packed, HALF, 0, pair, carries[0], query_part),
            put(grad_packed, HALF, D, pair, carries[1], key_part),
            put(grad_packed, HALF, 2 * D, pair, carries[2], value_part),
        )

    over_pairs(body, [(grad_packed, HALF, base) for base in (0, D, 2 * D)])


def own_keys(scores, lane_block):
    kept = pick(scores[:FRAMES], lane_block == 0)
    for block in range(1, 8):
        kept = jnp.where(
            lane_block == block, scores[FRAMES * block : FRAMES * (block + 1)], kept
        )
    return kept


def all_keys(kept, lane_block):
    return jnp.concatenate([pick(kept, lane_block == block) for block in range(8)], axis=0)


def temporal_forward(packed, mixed, probs, group):
    rows = slice(group * HW, group * HW + HW)

    def body(pair, carries):
        masks = pair_masks(pair)
        lane_block = lax.broadcasted_iota(jnp.int32, (1, 256), 1) // FRAMES
        queries = half(packed, group, window(pair))
        keys = half(packed, group, window(pair, D))
        values = half(packed, group, window(pair, 2 * D))
        weights = []
        for index, mask in enumerate(masks):
            weight = softmax_keys(own_keys(nt(pick(keys, mask), queries), lane_block)).astype(BF16)
            probs[group * HEADS + 2 * pair + index] = weight
            weights.append(all_keys(weight, lane_block))
        result = tn(
            jnp.concatenate(weights, axis=0),
            jnp.concatenate([pick(values, mask) for mask in masks], axis=0),
        )
        return (put(mixed, rows, 0, pair, carries[0], result),)

    over_pairs(body, [(mixed, rows, 0)])


def temporal_backward(packed, grad_mixed, grad_packed, probs, group):
    def body(pair, carries):
        masks = pair_masks(pair)
        lane_block = lax.broadcasted_iota(jnp.int32, (1, 256), 1) // FRAMES
        queries = half(packed, group, window(pair))
        keys = half(packed, group, window(pair, D))
        values = half(packed, group, window(pair, 2 * D))
        grads = [pick(half(grad_mixed, group, window(pair)), mask) for mask in masks]
        weights, scores = [], []
        for index, grad in enumerate(grads):
            weight = probs[group * HEADS + 2 * pair + index]
            grad_attention = own_keys(nt(values, grad), lane_block)
            wide = weight.astype(F32)
            inner = jnp.sum(wide * grad_attention, axis=0, keepdims=True)
            score = (wide * (grad_attention - inner) * SCALE).astype(BF16)
            weights.append(all_keys(weight, lane_block))
            scores.append(all_keys(score, lane_block))
        value_part = nn(jnp.concatenate(weights, axis=1), jnp.concatenate(grads, axis=0))
        query_part = tn(
            jnp.concatenate(scores, axis=0),
            jnp.concatenate([pick(keys, mask) for mask in masks], axis=0),
        )
        key_part = nn(
            jnp.concatenate(scores, axis=1),
            jnp.concatenate([pick(queries, mask) for mask in masks], axis=0),
        )
        return (
            put(grad_packed, HALF, 0, pair, carries[0], query_part),
            put(grad_packed, HALF, D, pair, carries[1], key_part),
            put(grad_packed, HALF, 2 * D, pair, carries[2], value_part),
        )

    over_pairs(body, [(grad_packed, HALF, base) for base in (0, D, 2 * D)])


def weight_shares(left, right, part, ready):
    tail, at = None, 0
    for chunk in range(3):
        product = tn(left[:, 384 * chunk : 384 * chunk + 384], right[...])
        if tail is not None:
            product = jnp.concatenate([tail, product], axis=0)
        count = product.shape[0] // SHARE
        for index in range(count):
            share = product[SHARE * index : SHARE * index + SHARE]
            padding = jnp.zeros((PADDED - SHARE, D), F32)
            core, chip = (at + index) % 2, (at + index) // 2
            part[core, chip // 4, chip % 4] = jnp.concatenate([share, padding], axis=0).astype(BF16)
        for chip in range(at // 2, (at + count) // 2):
            ready(chip)
        at += count
        tail = product[SHARE * count :] if at < SEQ else None


def settle(ref, sem):
    pltpu.make_async_copy(ref, ref, sem).wait()


class Reduction:
    def __init__(self, part, first, sems):
        self.part, self.first = part, first
        self.first_send, self.first_recv = sems
        self.me = lax.axis_index("seq")
        self.clip = lax.axis_index("dp")
        self.core = lax.rem(self.me, 2)
        self.chip = self.me // 2
        self.along_x = lax.rem(self.clip, 4)
        self.along_y = self.clip // 4
        self.along_z = lax.rem(self.chip, 4)

    def copy(self, source, target, send, recv, device):
        return pltpu.make_async_remote_copy(
            src_ref=source,
            dst_ref=target,
            send_sem=send,
            recv_sem=recv,
            device_id=device,
            device_id_type=MESH,
        )

    def x_peer(self, step):
        return lax.rem(self.along_x + step, 4)

    def to_x(self, step, source, target, sems):
        device = {"dp": 4 * self.along_y + self.x_peer(step)}
        self.copy(source, target, sems.at[0], sems.at[1], device).start()

    def to_seq(self, step, source, target, sems):
        device = {"seq": 2 * lax.rem(self.chip + step, 8) + self.core}
        self.copy(source, target, sems.at[0], sems.at[1], device).start()

    def to_dp(self, step, place, sems):
        device = {"dp": lax.rem(self.clip + step, DP)}
        self.copy(place, place, sems.at[0], sems.at[1], device).start()

    def to_core(self, chip):
        return self.copy(
            self.part.at[1 - self.core, chip // 4, lax.rem(chip, 4)],
            self.first.at[chip // 4, lax.rem(chip, 4)],
            self.first_send,
            self.first_recv.at[chip],
            {"seq": self.me + 1 - 2 * self.core},
        )

    def start(self, left, right):
        weight_shares(left, right, self.part, lambda chip: self.to_core(chip).start())

    def add_cores(self, chip):
        self.to_core(chip).wait_recv()
        high, low = chip // 4, lax.rem(chip, 4)
        total = self.part[self.core, high, low].astype(F32) + self.first[high, low].astype(F32)
        self.part[self.core, high, low] = total.astype(BF16)

    def lanes(self, at, width):
        return pl.ds(pl.multiple_of(at, 128), width)

    def finish(self, out, factor):
        self.settle_all()
        total = self.final[0, :SHARE, :].astype(F32) + self.final[1, :SHARE, :].astype(F32)
        out[...] = total * factor


class TwoWays(Reduction):
    def __init__(self, part, first, wide, second, rest, block, third, last, final, sems, pairs):
        super().__init__(part, first, sems)
        self.wide, self.second, self.rest = wide, second, rest
        self.block, self.third, self.last, self.final = block, third, last, final
        (self.wide_sems, self.second_sems, self.rest_sems, self.third_sems, self.last_sems,
         self.final_sems, self.end_sems) = pairs

    def over_cores(self):
        def send(step, carry):
            chip = lax.rem(self.chip + step, 8)
            self.add_cores(chip)

            @pl.when(step < 8)
            def _():
                source = self.part.at[self.core, chip // 4, lax.rem(chip, 4), :, pl.ds(512, 640)]
                self.to_seq(step, source, self.rest.at[step], self.rest_sems)

            return carry

        lax.fori_loop(1, 9, send, 0)
        for step in range(1, 4):
            columns = self.lanes(128 * self.x_peer(step), 128)
            source = self.part.at[self.core, :, :, :, columns]
            self.to_x(step, source, self.wide.at[self.along_x], self.wide_sems)

    def second_stage(self):
        settle(self.wide.at[pl.ds(0, 3)], self.wide_sems.at[1])
        columns = self.lanes(128 * self.along_x, 128)
        total = self.part[self.core, :, :, :, columns].astype(F32)
        for step in range(1, 4):
            total = total + self.wide[self.x_peer(step)].astype(F32)
        self.wide[self.along_x] = total.astype(BF16)

        def send(step, carry):
            chip = lax.rem(self.chip + step, 8)
            source = self.wide.at[self.along_x, chip // 4, lax.rem(chip, 4)]
            self.to_seq(step, source, self.second.at[step], self.second_sems)
            return carry

        lax.fori_loop(1, 8, send, 0)

    def second_stage_rest(self):
        settle(self.rest.at[pl.ds(1, 7)], self.rest_sems.at[1])
        total = self.part[self.core, self.chip // 4, self.along_z, :, 512:1152].astype(F32)
        for step in range(1, 8):
            total = total + self.rest[step].astype(F32)
        self.block[...] = total.astype(BF16)
        columns = self.lanes(128 * self.along_x, 128)
        self.third[self.along_x] = self.block[:, columns]
        self.last[self.along_x] = self.block[:, 512:640]
        for step in range(1, 4):
            source = self.block.at[:, self.lanes(128 * self.x_peer(step), 128)]
            self.to_x(step, source, self.third.at[self.along_x], self.third_sems)
            source = self.block.at[:, pl.ds(512, 128)]
            self.to_x(step, source, self.last.at[self.along_x], self.last_sems)

    def third_stage(self):
        first = self.lanes(128 * self.along_x, 128)
        settle(self.second.at[pl.ds(1, 7)], self.second_sems.at[1])
        total = self.wide[self.along_x, self.chip // 4, self.along_z].astype(F32)
        for step in range(1, 8):
            total = total + self.second[step].astype(F32)
        self.final[self.along_y, :, first] = total.astype(BF16)
        for step in range(1, DP):
            self.to_dp(step, self.final.at[self.along_y, :, first], self.final_sems)

    def third_stage_rest(self):
        other = self.lanes(512 + 128 * self.along_x, 128)
        settle(self.third.at[pl.ds(0, 3)], self.third_sems.at[1])
        settle(self.last.at[pl.ds(0, 3)], self.last_sems.at[1])
        total, last = self.third[0].astype(F32), self.last[0].astype(F32)
        for source in range(1, 4):
            total = total + self.third[source].astype(F32)
            last = last + self.last[source].astype(F32)
        self.final[self.along_y, :, other] = total.astype(BF16)
        self.final[self.along_y, :, 1024:1152] = last.astype(BF16)
        for step in range(1, DP):
            self.to_dp(step, self.final.at[self.along_y, :, other], self.final_sems)
        self.to_dp(4, self.final.at[self.along_y, :, pl.ds(1024, 128)], self.end_sems)

    def settle_all(self):
        settle(self.rest.at[pl.ds(0, 7), :, pl.ds(0, 256)], self.final_sems.at[1])
        settle(self.second.at[0], self.end_sems.at[1])

    def drain(self):
        settle(self.first, self.first_send)
        settle(self.rest.at[pl.ds(1, 7)], self.rest_sems.at[0])
        settle(self.wide.at[pl.ds(0, 3)], self.wide_sems.at[0])
        settle(self.second.at[pl.ds(1, 7)], self.second_sems.at[0])
        settle(self.third.at[pl.ds(0, 3)], self.third_sems.at[0])
        settle(self.last.at[pl.ds(0, 3)], self.last_sems.at[0])
        settle(self.rest.at[pl.ds(0, 7), :, pl.ds(0, 256)], self.final_sems.at[0])
        settle(self.second.at[0], self.end_sems.at[0])


class RowsFirst(Reduction):
    def __init__(self, part, first, wide, wide_last, second, second_last, final, sems, pairs):
        super().__init__(part, first, sems)
        self.wide, self.wide_last = wide, wide_last
        self.second, self.second_last, self.final = second, second_last, final
        (self.wide_sems, self.wide_last_sems, self.second_sems, self.second_last_sems,
         self.final_sems, self.final_last_sems) = pairs

    def over_cores(self):
        def add(chip, carry):
            self.add_cores(chip)
            return carry

        lax.fori_loop(0, 8, add, 0)
        for step in range(1, 4):
            peer = self.x_peer(step)
            source = self.part.at[self.core, :, :, :, self.lanes(256 * peer, 256)]
            self.to_x(step, source, self.wide.at[self.along_x], self.wide_sems)
            source = self.part.at[self.core, :, peer, :, pl.ds(1024, 128)]
            self.to_x(step, source, self.wide_last.at[self.along_x], self.wide_last_sems)

    def with_last(self, step):
        return lax.rem(self.chip + step, 4) == self.along_x

    def over_x(self):
        settle(self.wide.at[pl.ds(0, 3)], self.wide_sems.at[1])
        settle(self.wide_last.at[pl.ds(0, 3)], self.wide_last_sems.at[1])
        for high in range(2):
            columns = self.lanes(256 * self.along_x, 256)
            total = self.part[self.core, high, :, :, columns].astype(F32)
            last = self.part[self.core, high, self.along_x, :, 1024:1152].astype(F32)
            for step in range(1, 4):
                total = total + self.wide[self.x_peer(step), high].astype(F32)
                last = last + self.wide_last[self.x_peer(step), high].astype(F32)
            self.wide[self.along_x, high] = total.astype(BF16)
            self.wide_last[self.along_x, high] = last.astype(BF16)

        def send(step, carry):
            chip = lax.rem(self.chip + step, 8)
            source = self.wide.at[self.along_x, chip // 4, lax.rem(chip, 4)]
            self.to_seq(step, source, self.second.at[step], self.second_sems)

            @pl.when(self.with_last(step))
            def _():
                source = self.wide_last.at[self.along_x, chip // 4]
                self.to_seq(step, source, self.second_last.at[step], self.second_last_sems)

            return carry

        lax.fori_loop(1, 8, send, 0)

    def over_seq(self):
        high = self.chip // 4
        columns = self.lanes(256 * self.along_x, 256)
        settle(self.second.at[pl.ds(1, 7)], self.second_sems.at[1])
        total = self.wide[self.along_x, high, self.along_z].astype(F32)
        for step in range(1, 8):
            total = total + self.second[step].astype(F32)
        self.final[self.along_y, :, columns] = total.astype(BF16)
        for step in range(1, DP):
            self.to_dp(step, self.final.at[self.along_y, :, columns], self.final_sems)

        @pl.when(self.along_z == self.along_x)
        def _():
            settle(self.second_last.at[pl.ds(1, 7)], self.second_last_sems.at[1])
            last = self.wide_last[self.along_x, high].astype(F32)
            for step in range(1, 8):
                last = last + self.second_last[step].astype(F32)
            self.final[self.along_y, :, 1024:1152] = last.astype(BF16)
            for step in range(1, DP):
                place = self.final.at[self.along_y, :, pl.ds(1024, 128)]
                self.to_dp(step, place, self.final_last_sems)

    def settle_all(self):
        settle(self.second.at[pl.ds(0, 7)], self.final_sems.at[1])

        @pl.when(self.along_z == self.along_x)
        def _():
            settle(self.second_last.at[0], self.final_last_sems.at[1])

        @pl.when(self.along_z != self.along_x)
        def _():
            settle(self.second_last.at[pl.ds(0, 2)], self.final_last_sems.at[1])

    def drain(self):
        settle(self.first, self.first_send)
        settle(self.wide.at[pl.ds(0, 3)], self.wide_sems.at[0])
        settle(self.wide_last.at[pl.ds(0, 3)], self.wide_last_sems.at[0])
        settle(self.second.at[pl.ds(1, 7)], self.second_sems.at[0])
        settle(self.second.at[pl.ds(0, 7)], self.final_sems.at[0])

        @pl.when(self.along_z == self.along_x)
        def _():
            settle(self.second_last.at[0], self.second_last_sems.at[0])
            settle(self.second_last.at[pl.ds(0, 7)], self.final_last_sems.at[0])

        @pl.when(self.along_z != self.along_x)
        def _():
            settle(self.second_last.at[pl.ds(0, 2)], self.second_last_sems.at[0])


def kernel(
    x_hbm, cot_hbm, sqkv_hbm, sout_hbm, tqkv_hbm, tout_hbm,
    grad_hbm, sgrad, tgrad,
    x, cot, qkv, sout, tout,
    packed, mixed, probs, temporal_probs, residual, residual_in, cot_in, mixed_in,
    res, cot_pos, packed_two, grad_mixed, mixed_two, grad_packed, grad_norm,
    back, back_in,
    t_part, t_first, t_wide, t_wide_last, t_second, t_second_last, t_final,
    s_part, s_first, s_wide, s_second, s_rest, s_block, s_third, s_last, s_final,
    load, swap, out_sem,
    cot_send, cot_recv, res_send, res_recv, back_send, back_recv, mixed_send, mixed_recv,
    *sems,
):
    me, clip = lax.axis_index("seq"), lax.axis_index("dp")
    temporal_sum = RowsFirst(
        t_part, t_first, t_wide, t_wide_last, t_second, t_second_last, t_final, sems[:2], sems[4:10]
    )
    spatial_sum = TwoWays(
        s_part, s_first, s_wide, s_second, s_rest, s_block, s_third, s_last, s_final,
        sems[2:4], sems[10:],
    )
    factor = 1.0 / math.sqrt(TOKENS * SEQ * DP)

    qkv_chunks = chunks(3 * D, 768)

    def load_qkv(source, index):
        at, size = qkv_chunks[index]
        columns = pl.ds(at, size)
        return pltpu.make_async_copy(source.at[:, columns], qkv.at[:, columns], swap.at[index])

    load_x = pltpu.make_async_copy(x_hbm, x, load.at[0])
    load_cot = pltpu.make_async_copy(cot_hbm, cot, load.at[1])
    load_sout = pltpu.make_async_copy(sout_hbm, sout, load.at[2])
    load_tout = pltpu.make_async_copy(tout_hbm, tout, load.at[3])
    load_x.start()
    load_cot.start()
    for index in range(len(qkv_chunks)):
        load_qkv(sqkv_hbm, index).start()
    load_sout.start()

    barrier = pltpu.get_barrier_semaphore()

    def greet_seq(step, carry):
        pl.semaphore_signal(
            barrier, inc=1, device_id={"seq": lax.rem(me + step, SEQ)}, device_id_type=MESH
        )
        return carry

    def greet_dp(step, carry):
        pl.semaphore_signal(
            barrier, inc=1, device_id={"dp": lax.rem(clip + step, DP)}, device_id_type=MESH
        )
        return carry

    lax.fori_loop(1, SEQ, greet_seq, 0)
    lax.fori_loop(1, DP, greet_dp, 0)

    def send_cot(peer, frame):
        return pltpu.make_async_remote_copy(
            src_ref=cot.at[frame, pl.ds(pl.multiple_of(16 * peer, 16), 16), :],
            dst_ref=cot_in.at[frame, me],
            send_sem=cot_send.at[frame],
            recv_sem=cot_recv.at[frame],
            device_id={"seq": peer},
            device_id_type=MESH,
        )

    def send_residual(peer, frame):
        return pltpu.make_async_remote_copy(
            src_ref=residual.at[frame, pl.ds(pl.multiple_of(16 * peer, 16), 16), :],
            dst_ref=residual_in.at[frame, me],
            send_sem=res_send.at[frame],
            recv_sem=res_recv.at[frame],
            device_id={"seq": peer},
            device_id_type=MESH,
        )

    def send_back(peer, group):
        return pltpu.make_async_remote_copy(
            src_ref=back.at[peer, group],
            dst_ref=back_in.at[me, group],
            send_sem=back_send.at[group],
            recv_sem=back_recv.at[group],
            device_id={"seq": peer},
            device_id_type=MESH,
        )

    def send_mixed(peer, frame):
        return pltpu.make_async_remote_copy(
            src_ref=mixed.at[pl.ds(pl.multiple_of(frame * HW + 16 * peer, 16), 16)],
            dst_ref=mixed_in.at[frame, me],
            send_sem=mixed_send.at[frame],
            recv_sem=mixed_recv.at[frame],
            device_id={"seq": peer},
            device_id_type=MESH,
        )

    def each(action):
        high, low, core = me // 8, lax.rem(me, 8) // 2, lax.rem(me, 2)
        for turn, count in ((2, 4), (1, 4), (3, 4), (0, 3)):

            def body(index, carry, turn=turn):
                chip = 4 * lax.rem(high + 1 - index // 2, 2) + lax.rem(low + turn, 4)
                action(2 * chip + lax.rem(core + 1 - lax.rem(index, 2), 2))
                return carry

            lax.fori_loop(0, count, body, 0)

    def exchanged(sem):
        settle(cot_in.at[0, pl.ds(0, SEQ - 1)], sem)

    load_x.wait()
    for frame in range(2):
        rows = slice(frame * HW, frame * HW + HW)
        norm, _ = rms_forward(x[frame])
        for index, (at, size) in enumerate(qkv_chunks):
            if frame == 0:
                load_qkv(sqkv_hbm, index).wait()
            if frame == 0 and index == 1:
                load_cot.wait()
                pl.semaphore_wait(barrier, SEQ - 1 + DP - 1)
                each(lambda peer: send_cot(peer, 0).start())
            packed[rows, at : at + size] = nn(norm, qkv[:, at : at + size]).astype(BF16)
        if frame == 0:
            cot_in[:, me] = cot[:, pl.ds(pl.multiple_of(16 * me, 16), 16), :]
        else:
            for index in range(len(qkv_chunks)):
                load_qkv(tqkv_hbm, index).start()
            load_tout.start()
        spatial_forward(packed, mixed, probs, frame)
        if frame == 0:
            load_sout.wait()
        for at, size in chunks(D, 256):
            residual[frame, :, at : at + size] = (
                x[frame, :, at : at + size].astype(F32) + nn(mixed[rows, :], sout[:, at : at + size])
            ).astype(BF16)
        each(lambda peer: send_residual(peer, frame).start())
        residual_in[frame, me] = residual[frame, pl.ds(pl.multiple_of(16 * me, 16), 16), :]

    each(lambda peer: send_cot(peer, 1).start())
    for frame in range(2):
        each(lambda peer: send_mixed(peer, frame).start())
        mixed_in[frame, me] = mixed[pl.ds(pl.multiple_of(frame * HW + 16 * me, 16), 16), :]

    by_position = one_hot(HW, HW, lambda row: (row % SEQ) * 16 + row // SEQ)

    def positions(source, parity):
        return nn(by_position, source[parity].reshape(HW, D)).astype(BF16)

    def spread(values):
        return values.astype(BF16).reshape(16, SEQ, -1)

    def grads_of_mixed(parity):
        exchanged(cot_recv.at[parity])
        rows = positions(cot_in, parity)
        cot_pos[:, parity] = spread(rows)
        for at, size in chunks(D, 256):
            grad_mixed[:, parity, :, at : at + size] = spread(nt(rows, tout[at : at + size, :]))

    for parity in range(2):
        exchanged(res_recv.at[parity])
        rows = positions(residual_in, parity)
        res[:, parity] = spread(rows)
        norm, _ = rms_forward(rows)
        for index, (at, size) in enumerate(qkv_chunks):
            if parity == 0:
                load_qkv(tqkv_hbm, index).wait()
            packed_two[:, parity, :, at : at + size] = spread(nn(norm, qkv[:, at : at + size]))
        if parity == 0:
            load_tout.wait()
            grads_of_mixed(0)
    for group in range(2):
        temporal_forward(packed_two, mixed_two, temporal_probs, group)

    grads_of_mixed(1)
    temporal_sum.start(mixed_two, cot_pos[...].reshape(TOKENS, D))
    for group in range(2):
        temporal_backward(packed_two, grad_mixed, grad_packed, temporal_probs, group)
        if group == 0:
            temporal_sum.over_cores()
        for at, size in chunks(D, 256):
            grad_norm[:, at : at + size] = nt(grad_packed[...], qkv[at : at + size, :]).astype(BF16)
        if group == 1:
            for index in range(len(qkv_chunks)):
                load_qkv(sqkv_hbm, index).start()
        rows = half(res, group)
        _, inverse = rms_forward(rows)
        grad = (
            half(cot_pos, group).astype(F32) + rms_backward(rows, grad_norm[...], inverse)
        ).astype(BF16)
        order = one_hot(
            HW, HW, lambda row: (row % 8) * FRAMES + ((row // 8) % 2) * 16 + row // 16
        )
        back[:, group] = nn(order, grad).astype(BF16).reshape(SEQ, 16, D)
        each(lambda peer: send_back(peer, group).start())
        back_in[me, group] = back[me, group]
        grad_mixed[8 * group : 8 * group + 8] = grad.reshape(8, 2, SEQ, D)

    for frame in range(2):
        exchanged(mixed_recv.at[frame])
    for group in range(2):
        rows = slice(group * HW, group * HW + HW)
        order = one_hot(
            HW,
            TOKENS,
            lambda row, group=group: (
                (row // 16) % 2 * HW + (row % 16) * 16 + group * 8 + row // FRAMES
            ),
        )
        mixed_two[rows, :] = nn(order, mixed_in[...].reshape(TOKENS, D)).astype(BF16)
    spatial_sum.start(mixed_two, grad_mixed[...].reshape(TOKENS, D))
    temporal_sum.over_x()
    spatial_sum.over_cores()

    grad_res, grad_out = res, mixed_two
    for group in range(2):
        exchanged(back_recv.at[group])
    for frame in range(2):
        rows = slice(frame * HW, frame * HW + HW)
        order = one_hot(HW, TOKENS, lambda row, frame=frame: (row // 8) * 16 + frame * 8 + row % 8)
        grad_res[8 * frame : 8 * frame + 8] = (
            nn(order, back_in[...].reshape(TOKENS, D)).astype(BF16).reshape(8, 2, SEQ, D)
        )

    def store(frame):
        return pltpu.make_async_copy(
            grad_out.at[pl.ds(frame * HW, HW)], grad_hbm.at[frame], out_sem.at[frame]
        )

    for at, size in chunks(D, 256):
        product = nt(grad_res[...].reshape(TOKENS, D), sout[at : at + size, :])
        grad_mixed[:, :, :, at : at + size] = product.astype(BF16).reshape(16, 2, SEQ, size)
    for index in range(len(qkv_chunks)):
        load_qkv(sqkv_hbm, index).wait()
    for frame in range(2):
        rows = slice(frame * HW, frame * HW + HW)
        spatial_backward(packed, grad_mixed, grad_packed, probs, frame)
        if frame == 1:
            spatial_sum.second_stage_rest()
        for at, size in chunks(D, 256):
            grad_norm[:, at : at + size] = nt(grad_packed[...], qkv[at : at + size, :]).astype(BF16)
        _, inverse = rms_forward(x[frame])
        grad_out[rows, :] = (
            half(grad_res, frame).astype(F32) + rms_backward(x[frame], grad_norm[...], inverse)
        ).astype(BF16)
        store(frame).start()
        if frame == 0:
            spatial_sum.second_stage()
            temporal_sum.over_seq()

    spatial_sum.third_stage()
    temporal_sum.finish(tgrad, factor)
    spatial_sum.third_stage_rest()
    temporal_sum.drain()
    for frame in range(2):
        store(frame).wait()
        exchanged(cot_send.at[frame])
        exchanged(res_send.at[frame])
        exchanged(back_send.at[frame])
        exchanged(mixed_send.at[frame])
    spatial_sum.finish(sgrad, factor)
    spatial_sum.drain()


def local(layer_input, cotangent, spatial_qkv, spatial_out, temporal_qkv, temporal_out):
    def vmem(*shape, dtype=BF16):
        return pltpu.VMEM(shape, dtype)

    by_rows = [
        vmem(2, 2, 4, PADDED, D), vmem(2, 4, PADDED, D),
        vmem(4, 2, 4, PADDED, 256), vmem(4, 2, PADDED, 128),
        vmem(8, PADDED, 256), vmem(8, PADDED, 128), vmem(2, PADDED, D),
    ]
    two_ways = [
        vmem(2, 2, 4, PADDED, D), vmem(2, 4, PADDED, D),
        vmem(4, 2, 4, PADDED, 128), vmem(8, PADDED, 128), vmem(8, PADDED, 640),
        vmem(PADDED, 640), vmem(4, PADDED, 128), vmem(4, PADDED, 128), vmem(2, PADDED, D),
    ]
    dma = pltpu.SemaphoreType.DMA
    scratch = [
        vmem(2, HW, D), vmem(2, HW, D), vmem(D, 3 * D), vmem(D, D), vmem(D, D),
        vmem(TOKENS, 3 * D), vmem(TOKENS, D), vmem(2 * HEADS, HW, HW), vmem(2 * HEADS, FRAMES, HW),
        vmem(2, HW, D), *[vmem(2, SEQ, 16, D) for _ in range(3)],
        vmem(16, 2, SEQ, D), vmem(16, 2, SEQ, D), vmem(16, 2, SEQ, 3 * D), vmem(16, 2, SEQ, D),
        vmem(TOKENS, D), vmem(HW, 3 * D), vmem(HW, D),
        vmem(SEQ, 2, 16, D), vmem(SEQ, 2, 16, D),
        *by_rows,
        *two_ways,
        dma((4,)), dma((5,)), dma((2,)),
        *[dma((2,)) for _ in range(8)],
        *[dma(()), dma((8,))] * 2,
        *[dma((2,)) for _ in range(13)],
    ]
    hbm, on_chip = pl.BlockSpec(memory_space=pl.ANY), pl.BlockSpec(memory_space=pltpu.VMEM)
    grad, spatial_grad, temporal_grad = pl.pallas_call(
        kernel,
        out_shape=(
            jax.ShapeDtypeStruct((2, HW, D), BF16),
            jax.ShapeDtypeStruct((SHARE, D), F32),
            jax.ShapeDtypeStruct((SHARE, D), F32),
        ),
        in_specs=[hbm] * 6,
        out_specs=(hbm, on_chip, on_chip),
        scratch_shapes=scratch,
        compiler_params=pltpu.CompilerParams(
            collective_id=0, has_side_effects=True, vmem_limit_bytes=62 * 2**20
        ),
        cost_estimate=pl.CostEstimate(
            flops=40_000_000_000, bytes_accessed=40_000_000, transcendentals=3_000_000
        ),
        name="attention_pair_backward",
    )(
        layer_input.reshape(2, HW, D), cotangent.reshape(2, HW, D),
        spatial_qkv, spatial_out, temporal_qkv, temporal_out,
    )
    return grad.reshape(1, 2, HW, D), spatial_grad, temporal_grad


def solution(mesh):
    placed = (P("dp", "seq", None, None), P("dp", "seq", None, None), P(), P(), P(), P())
    return jax.shard_map(
        local,
        mesh=mesh,
        in_specs=placed,
        out_specs=(P("dp", "seq", None, None), P("seq", None), P("seq", None)),
        check_vma=False,
    )
```
